256 devices in a mesh: mp: 2 (over x_lo), tok: 16 (over z, core), vocab: 8 (over x_hi, y).
Axes of the slice: x: 4 (x_hi: 2, x_lo: 2; x = x_hi * 2 + x_lo), y: 4, z: 8, core: 2. Of those that a mesh axis runs over, the one named last changes fastest.
Arguments:
- hidden: bfloat16 [2, 128, 5120], P('mp', 'tok'), may hold values from -400 to 400
- norm_gain: float32 [2, 5120], P('mp'), may hold values from 0.5 to 1.5
- output_head: bfloat16 [2, 76800, 5120], P('mp', 'vocab', 'tok'), may hold values from -0.703125 to 0.703125
- token_ids: int32 [128], P('tok'), may hold values from 0 to 76799
- live_mask: int32 [128], P('tok'), may hold values from 0 to 1, as said below
- advantages: float32 [128], P('tok'), may hold values from -4 to 4
Outputs:
- hidden_grad: float32 [128, 5120], P('tok', 'mp')
- head_grad: bfloat16 [2, 38400, 5120], P('mp', 'vocab', 'tok')
The draws below stay inside these ranges and needn't reach their ends.
Inputs may be any that keep to these rules, and one draw needn't show every extreme that they name: `live_mask`: 1 marks a response token, 0 a masked one; the last token is live.
All inputs are finite; a program needn't handle non-finite values.
Results may differ from the reference program's by a relative error of at most 0.0044.
The reference program's roundings to bfloat16 on the way (of `normed` and `logit_grad`) count: a program that leaves them out, or rounds other values in their place, can miss the bound.
Values may be sent and summed in bfloat16 or wider, within the bound.
A program may use at most 64 MiB of HBM per device.

```python
import math
import jax
import jax.numpy as jnp
import numpy as np
from jax import lax

D = 5120
VOCAB = 76800
TOKENS = 128
HALF = 4800
N_VOCAB = 8


def shared_hidden(key):
    base = jax.random.truncated_normal(key, -4.0, 4.0, (2, TOKENS, D), jnp.float32)
    column_scale = jnp.exp(jax.random.uniform(jax.random.fold_in(key, 11), (2, 1, D), jnp.float32) * math.log(10.0))
    return base * column_scale


def draw_hidden(key, part):
    scaled_cols = shared_hidden(key)
    key = jax.random.fold_in(key, 3)
    row_scale = jnp.exp(jax.random.uniform(key, (2, TOKENS, 1), jnp.float32) * math.log(10.0))
    return (scaled_cols * row_scale).astype(jnp.bfloat16)


def draw_output_head(key, part):
    key = jax.random.fold_in(key, 7)
    weights = 0.045 * jax.random.truncated_normal(key, -4.0, 4.0, (2, VOCAB, D), jnp.float32)
    return weights.astype(jnp.bfloat16)


def draw_live_mask(key, part):
    key = jax.random.fold_in(key, 5)
    position = jnp.arange(TOKENS, dtype=jnp.int32)
    ticket = jax.random.randint(key, (TOKENS,), 0, 4 * TOKENS, dtype=jnp.int32)
    return jnp.where((ticket < TOKENS + 2 * position) | (position == TOKENS - 1), 1, 0).astype(jnp.int32)


def with_ends(entries, key, low, high):
    extent = entries.shape
    spot = [jax.random.randint(jax.random.fold_in(key, axis), (), 0, extent[axis]) for axis in range(len(extent))]
    entries = entries.at[tuple(spot)].set(low)
    longest = extent.index(max(extent))
    spot[longest] = (spot[longest] + 1) % extent[longest]
    return entries.at[tuple(spot)].set(high)


def block_scale(key, extent, split, smallest, largest):
    def one(dim, parts):
        steps = jax.random.uniform(jax.random.fold_in(jax.random.fold_in(key, 6), dim), (parts,), jnp.float32, smallest / len(split), largest / len(split))
        return jnp.repeat(jnp.exp(steps), extent[dim] // parts).reshape((-1,) + (1,) * (len(extent) - dim - 1))

    level = one(*split[0])
    for cut in split[1:]:
        level = level * one(*cut)
    return level


def ranked_wide(key, shape, amount, slope):
    weights = [min(1 << octave, amount + 1 - (1 << octave)) * (1 << 20) // math.isqrt((1 << octave) ** slope) + 1 for octave in range((amount + 1).bit_length()) if 1 << octave <= amount]
    scale = 1 + sum(weights) // (1 << 30)
    table = np.cumsum(np.array([max(1, weight // scale) for weight in weights]))
    ticket = jax.random.randint(jax.random.fold_in(key, 1), shape, 0, int(table[len(weights) - 1]))
    start = jnp.left_shift(1, jnp.searchsorted(jnp.asarray(table, jnp.int32), ticket, side="right").astype(jnp.int32))
    rank = start - 1 + jax.random.randint(jax.random.fold_in(key, 4), shape, 0, 1 << 30) % jnp.minimum(start, amount + 1 - start)
    return jax.random.permutation(jax.random.fold_in(key, 2), amount)[rank].astype(jnp.int32)


def centred(stream_key, shape, spread, bound, shards=(), held_as=jnp.bfloat16):
    gain = block_scale(stream_key, shape, shards, -0.22, 0.18) if shards else 1.0
    result = jax.random.normal(stream_key, shape, jnp.float32) * spread * gain
    return jnp.minimum(jnp.maximum(result, -bound), bound).astype(held_as)


def setup_inputs(seed: int = 0) -> dict:
    seeds = jax.random.split(jax.random.key(seed), 7)
    hidden = draw_hidden(jax.random.fold_in(seeds[6], 71), 0)
    norm_gain = jnp.clip(1.0 + 0.1 * jax.random.normal(seeds[1], (2, D), jnp.float32), 0.5, 1.5)
    output_head = draw_output_head(jax.random.fold_in(seeds[6], 71), 0)
    token_ids = with_ends(ranked_wide(seeds[3], (TOKENS,), VOCAB, 2), jax.random.fold_in(seeds[3], 3), 0, VOCAB - 1).astype(jnp.int32)
    live_mask = draw_live_mask(jax.random.fold_in(seeds[6], 71), 0)
    advantages = centred(seeds[5], (TOKENS,), 1.0, 4.0, ((0, 16),), jnp.float32)
    return {"hidden": hidden, "norm_gain": norm_gain, "output_head": output_head, "token_ids": token_ids, "live_mask": live_mask, "advantages": advantages}


loss_scale = 256.0
kl_coef = 0.1
norm_eps = 1e-06

def log_probs(logits):
    row_high = lax.optimization_barrier(jnp.max(logits, axis=1, keepdims=True))
    row_total = lax.optimization_barrier(jnp.sum(jnp.exp(logits - row_high), axis=1, keepdims=True))
    return logits - (row_high + jnp.log(row_total))

def reference(hidden, norm_gain, output_head, token_ids, live_mask, advantages):
    values = hidden.astype(jnp.float32)
    inv_rms = lax.rsqrt(lax.optimization_barrier(jnp.mean(values * values, axis=2, keepdims=True)) + norm_eps)
    unit_rows = values * inv_rms
    normed = (unit_rows * norm_gain[:, None, :]).astype(jnp.bfloat16)
    contract = (((1,), (1,)), ((), ()))
    policy_lp = log_probs(lax.dot_general(normed[0], output_head[0], contract, preferred_element_type=jnp.float32))
    ref_lp = log_probs(lax.dot_general(normed[1], output_head[1], contract, preferred_element_type=jnp.float32))
    lp_diff = policy_lp - ref_lp
    policy_prob = jnp.exp(policy_lp)
    kl_rows = lax.optimization_barrier(jnp.sum(policy_prob * lp_diff, axis=1, keepdims=True))
    live_f = live_mask.astype(jnp.float32)
    token_coef = (loss_scale * live_f / jnp.sum(live_f))[:, None]
    onehot = (lax.broadcasted_iota(jnp.int32, (1, VOCAB), 1) == token_ids.astype(jnp.int32)[:, None]).astype(jnp.float32)
    logit_grad = (token_coef * (advantages[:, None] * (policy_prob - onehot) + kl_coef * policy_prob * (lp_diff - kl_rows))).astype(jnp.bfloat16)
    feature_grad = jnp.dot(logit_grad, output_head[0], preferred_element_type=jnp.float32)
    head_grad = lax.dot_general(logit_grad, normed[0], (((0,), (0,)), ((), ())), preferred_element_type=jnp.float32).astype(jnp.bfloat16)
    head_grad = head_grad.reshape(N_VOCAB, 2, HALF, D).transpose(1, 0, 2, 3).reshape(2, VOCAB // 2, D)
    scaled = feature_grad * norm_gain[0]
    unit_pol = unit_rows[0]
    hidden_grad = inv_rms[0] * (scaled - unit_pol * lax.optimization_barrier(jnp.mean(unit_pol * scaled, axis=1, keepdims=True)))
    return (hidden_grad, head_grad)
```

```python
import functools

import jax
import jax.numpy as jnp
from jax import lax
from jax.experimental import pallas as pl
from jax.experimental.pallas import tpu as pltpu
from jax.sharding import PartitionSpec as P

loss_scale = 256.0
kl_coef = 0.1
norm_eps = 1e-06
MESH = pl.DeviceIdType.MESH
f32 = jnp.float32
bf16 = jnp.bfloat16


class Sems:
    def __init__(self):
        self.count = 0

    def take(self, number):
        first = self.count
        self.count += number
        return first


def sem_plan(nt, nz, nv):
    sems = Sems()
    half = nz // 2
    ring = 2 + 4 * (half - 1)
    plan = dict(
        a2a=sems.take(nt), meta=sems.take(nt), dw=sems.take(1), unit=sems.take(1), inv=sems.take(1),
        pair=sems.take(nz), up=sems.take(ring), down=sems.take(ring), peer=sems.take(4),
        tstat=sems.take(nt), vstat=sems.take(nv),
        gup=sems.take(2 * half - 1), gdown=sems.take(2 * half - 1), gpair=sems.take(2 * nz),
        fa=sems.take(nt), fr=sems.take(nv), fb=sems.take(2 * nv),
    )
    return plan, sems.count


def kernel(nt, nz, nv, plan, n_sem,
           hidden, gain, head, ids, live, adv,
           hg_out, head_out,
           wbuf, lbuf, xbuf, rbuf, ybuf, gbuf, hbuf,
           nbuf, cbuf, ubuf, urecv, ibuf, irecv, gainb, mbuf, colb, dwb,
           tst, vst, fbuf, fabuf, frbuf, fbb,
           wsem, hsem, ss, rs):
    mp = lax.axis_index("mp")
    tok = lax.axis_index("tok")
    voc = lax.axis_index("vocab")
    zi = tok // 2
    core = tok % 2
    sib = tok + 1 - 2 * core
    half = nz // 2
    T = nt * 8
    chip_rows = wbuf.shape[1]
    width = wbuf.shape[2]
    R = xbuf.shape[1]
    off = chip_rows - R
    over = R - off
    Q = R // 4
    H2 = R // 2
    spv = nt // nv
    pending = []

    def rcopy(src, dst, name, index, dev):
        at = plan[name] + index
        return pltpu.make_async_remote_copy(
            src_ref=src, dst_ref=dst, send_sem=ss.at[at], recv_sem=rs.at[at],
            device_id=dev, device_id_type=MESH)

    def zat(o):
        return lax.rem(zi + o + nz, nz)

    def up_dev():
        return {"tok": lax.rem(tok + 2, nt)}

    def down_dev():
        return {"tok": lax.rem(tok + nt - 2, nt)}

    def sib_dev():
        return {"tok": sib}

    order = [half]
    for d in range(half - 1, 0, -1):
        order += [d, -d]
    order += [0]

    def wcopy(k):
        z = zat(order[k])
        return pltpu.make_async_copy(
            head.at[0, pl.ds(pl.multiple_of(z * chip_rows, 16), chip_rows), :], wbuf.at[z], wsem.at[k])

    for k in range(nz):
        wcopy(k).start()

    barrier = pltpu.get_barrier_semaphore()

    @pl.loop(1, nt)
    def _(j):
        pl.semaphore_signal(barrier, inc=1, device_id={"tok": lax.rem(tok + j, nt)}, device_id_type=MESH)

    @pl.loop(1, nv)
    def _(j):
        pl.semaphore_signal(barrier, inc=1, device_id={"vocab": lax.rem(voc + j, nv)}, device_id_type=MESH)

    @pl.loop(0, nv)
    def _(j):
        pl.semaphore_signal(
            barrier, inc=1, device_id={"mp": 1 - mp, "vocab": lax.rem(voc + j, nv)}, device_id_type=MESH)

    x = hidden[0].astype(f32)
    inv = lax.rsqrt(jnp.mean(x * x, axis=1, keepdims=True) + norm_eps)
    unit = x * inv
    g = gain[...]
    normed = (unit * g).astype(bf16).astype(f32)
    for k in range(nt):
        cols = slice(k * width, (k + 1) * width)
        nbuf[k] = normed[:, cols]
        ubuf[k] = unit[:, cols]
        gainb[k] = jnp.broadcast_to(g[:, cols], (8, width))
    ibuf[...] = jnp.broadcast_to(inv, ibuf.shape)

    lane = lax.broadcasted_iota(jnp.int32, (8, T), 1)
    row = lax.broadcasted_iota(jnp.int32, (8, T), 0)
    id_row = jnp.zeros((8, T), jnp.int32)
    live_row = jnp.zeros((8, T), jnp.int32)
    adv_row = jnp.zeros((8, T), f32)
    for j in range(8):
        here = lane == tok * 8 + j
        id_row = jnp.where(here, ids[j], id_row)
        live_row = jnp.where(here, live[j], live_row)
        adv_row = jnp.where(here, adv[j], adv_row)
    mbuf[tok] = jnp.where(row == 0, id_row.astype(f32), jnp.where(row == 1, live_row.astype(f32), adv_row))
    cbuf[tok] = nbuf[tok]

    pl.semaphore_wait(barrier, nt - 1 + nv - 1 + nv)

    def a2a_copy(j):
        p = lax.rem(tok + j, nt)
        return rcopy(nbuf.at[p], cbuf.at[tok], "a2a", j, {"tok": p})

    def meta_copy(j):
        p = lax.rem(tok + j, nt)
        return rcopy(mbuf.at[tok], mbuf.at[tok], "meta", j, {"tok": p})

    @pl.loop(1, nt)
    def _(j):
        a2a_copy(j).start()

    @pl.loop(1, nt)
    def _(j):
        a2a_copy(j).wait_recv()

    colb[...] = cbuf[...].reshape(T, width).astype(bf16)

    def logits(k):
        z = zat(order[k])
        wcopy(k).wait()
        lbuf[z] = lax.dot_general(
            wbuf[z], colb[...], (((1,), (1,)), ((), ())), preferred_element_type=f32)
        other = pl.multiple_of((1 - core) * off, 8)
        c = rcopy(lbuf.at[z, pl.ds(other, R), :], xbuf.at[z], "pair", k, sib_dev())
        c.start()
        pending.append(c)
        return c

    def pair_add(k, c):
        z = zat(order[k])
        c.wait_recv()
        xbuf[z] = xbuf[z] + lbuf[z, pl.ds(pl.multiple_of(core * off, 8), R), :]

    def ring_list(first_pieces, rest):
        out = [(half, q) for q in first_pieces]
        for d in range(half - 1, 0, -1):
            out += [(d, q) for q in rest(d)]
        return out

    up_list = ring_list((0, 1), lambda d: (2, 3, 0, 1))
    down_list = ring_list((2, 3), lambda d: (2, 3, 0, 1) if d < 3 else (0, 1, 2, 3))
    slot = {}
    for i, m in enumerate(up_list):
        slot[("up",) + m] = i
    for i, m in enumerate(down_list):
        slot[("down",) + m] = i
    ring_len = len(up_list)

    def ring_copy(way, d, q):
        z = zat(d if way == "up" else -d)
        i = slot[(way, d, q)]
        return rcopy(
            xbuf.at[z, pl.ds(q * Q, Q), :], rbuf.at[i if way == "up" else ring_len + i], way, i,
            up_dev() if way == "up" else down_dev())

    def ring_send(way, d, q):
        c = ring_copy(way, d, q)
        c.start()
        pending.append(c)

    def has(way, d, q):
        return (way, d, q) in slot

    def arrived(way, d, q):
        ring_copy(way, d, q).wait_recv()
        i = slot[(way, d, q)]
        return rbuf[i if way == "up" else ring_len + i]

    ready = []
    for k in range(nz):
        ready.append(logits(k))
        if k >= 1:
            pair_add(k - 1, ready[k - 1])
            o = order[k - 1]
            if o == half:
                for q in (0, 1):
                    ring_send("up", half, q)
                    ring_send("down", half, q + 2)
            elif o == half - 1 and o > 0:
                for q in (2, 3):
                    ring_send("up", o, q)
            elif o == -(half - 1) and o < 0:
                for q in (0, 1):
                    ring_send("down", -o, q)
    pair_add(nz - 1, ready[nz - 1])

    dw_copy = rcopy(colb, dwb, "dw", 0, {"mp": 1 - mp})
    unit_copy = rcopy(ubuf.at[pl.ds(nt // 2, nt // 2)], urecv, "unit", 0, {"mp": 1 - mp})
    inv_copy = rcopy(ibuf, irecv, "inv", 0, {"mp": 1 - mp})
    for c in (dw_copy, unit_copy, inv_copy):
        c.start()
        pending.append(c)

    @pl.loop(1, nt)
    def _(j):
        meta_copy(j).start()

    def step(way, d, q):
        r = arrived(way, d, q)
        z = zat(d - 1 if way == "up" else 1 - d)
        rows = pl.ds(q * Q, Q)
        xbuf[z, rows, :] = xbuf[z, rows, :] + r
        if d > 1:
            ring_send(way, d - 1, q)

    def peer_copy(q):
        return rcopy(xbuf.at[zi, pl.ds(q * Q, Q), :], ybuf.at[pl.ds(q * Q, Q), :], "peer", q, {"mp": 1 - mp})

    for mu, md in zip(up_list, down_list):
        step("up", *mu)
        step("down", *md)
        if mu[0] == 1:
            c = peer_copy(mu[1])
            c.start()
            pending.append(c)

    @pl.loop(1, nt)
    def _(j):
        meta_copy(j).wait_recv()

    meta = jnp.sum(mbuf[...], axis=0)
    id_all = meta[0:1].astype(jnp.int32)
    live_all = meta[1:2]
    adv_all = meta[2:3]
    coef = loss_scale * live_all / jnp.sum(live_all)

    for q in (2, 3, 0, 1):
        peer_copy(q).wait_recv()

    own = xbuf[zi]
    peer = ybuf[...]
    l0 = jnp.where(mp == 0, own, peer)
    l1 = jnp.where(mp == 0, peer, own)
    rid = lax.broadcasted_iota(jnp.int32, (R, 1), 0)
    counted = jnp.where((rid >= over) | (core == 0), 1.0, 0.0).astype(f32)

    def tile_of(rows):
        out = jnp.zeros((8, T), f32)
        for i, r in enumerate(rows):
            out = jnp.where(row == i, r, out)
        return out

    h0 = jnp.max(l0, axis=0, keepdims=True)
    h1 = jnp.max(l1, axis=0, keepdims=True)
    e0 = jnp.exp(l0 - h0) * counted
    e1 = jnp.exp(l1 - h1) * counted
    tst[tok] = tile_of([
        h0, jnp.sum(e0, axis=0, keepdims=True), jnp.sum(e0 * (l0 - l1), axis=0, keepdims=True),
        h1, jnp.sum(e1, axis=0, keepdims=True)])

    def tstat_copy(j):
        return rcopy(tst.at[tok], tst.at[tok], "tstat", j, {"tok": lax.rem(tok + j, nt)})

    def vstat_copy(j):
        return rcopy(vst.at[voc], vst.at[voc], "vstat", j, {"vocab": lax.rem(voc + j, nv)})

    def combined(b):
        s = b[...]
        m0, s0, t0, m1, s1 = (s[:, i, :] for i in range(5))
        h0 = jnp.max(m0, axis=0, keepdims=True)
        h1 = jnp.max(m1, axis=0, keepdims=True)
        w0 = jnp.exp(m0 - h0)
        w1 = jnp.exp(m1 - h1)
        return [h0, jnp.sum(s0 * w0, axis=0, keepdims=True), jnp.sum(t0 * w0, axis=0, keepdims=True),
                h1, jnp.sum(s1 * w1, axis=0, keepdims=True)]

    @pl.loop(1, nt)
    def _(j):
        tstat_copy(j).start()

    @pl.loop(1, nt)
    def _(j):
        tstat_copy(j).wait_recv()

    vst[voc] = tile_of(combined(tst))

    @pl.loop(1, nv)
    def _(j):
        vstat_copy(j).start()

    @pl.loop(1, nv)
    def _(j):
        vstat_copy(j).wait_recv()

    h0, s0, t0, h1, s1 = combined(vst)
    lse0 = h0 + jnp.log(s0)
    lse1 = h1 + jnp.log(s1)
    kl = t0 / s0 - (lse0 - lse1)

    lp0 = l0 - lse0
    diff = lp0 - (l1 - lse1)
    prob = jnp.exp(lp0)
    entry = voc * (nz * chip_rows) + zi * chip_rows + core * off + rid
    onehot = jnp.where(entry == id_all, 1.0, 0.0).astype(f32)
    gbuf[core, zi] = (coef * (adv_all * (prob - onehot) + kl_coef * prob * (diff - kl))).astype(bf16)

    gup = [(s, h) for s in range(1, half) for h in (0, 1)] + [(half, 0)]
    gdown = [(s, h) for s in range(1, half) for h in (0, 1)] + [(half, 1)]

    def gring(way, s, h):
        z = zat(1 - s if way == "gup" else s - 1)
        view = gbuf.at[core, z, pl.ds(h * H2, H2), :]
        return rcopy(view, view, way, (gup if way == "gup" else gdown).index((s, h)),
                     up_dev() if way == "gup" else down_dev())

    def gring_recv(way, s, h):
        z = zat(-s if way == "gup" else s)
        view = gbuf.at[core, z, pl.ds(h * H2, H2), :]
        return rcopy(view, view, way, (gup if way == "gup" else gdown).index((s, h)),
                     up_dev() if way == "gup" else down_dev())

    def gpair(o, h):
        view = gbuf.at[core, zat(o), pl.ds(h * H2, H2), :]
        return rcopy(view, view, "gpair", 2 * (o % nz) + h, sib_dev())

    def gpair_recv(o, h):
        view = gbuf.at[1 - core, zat(o), pl.ds(h * H2, H2), :]
        return rcopy(view, view, "gpair", 2 * (o % nz) + h, sib_dev())

    def begin(c):
        c.start()
        pending.append(c)

    for h in (0, 1):
        if (1, h) in gup:
            begin(gring("gup", 1, h))
        if (1, h) in gdown:
            begin(gring("gdown", 1, h))
    for h in (0, 1):
        begin(gpair(0, h))

    def feature(o):
        for h in (0, 1):
            gpair_recv(o, h).wait_recv()

        @pl.when(mp == 0)
        def _():
            z = zat(o)
            tn = (((0,), (0,)), ((), ()))
            part = lax.dot_general(
                gbuf[0, z], wbuf[z, 0:R, :], tn, preferred_element_type=f32)
            part = part + lax.dot_general(
                gbuf[1, z, over:R, :], wbuf[z, R:chip_rows, :], tn, preferred_element_type=f32)
            part = part.reshape(nt, 8, width)
            if o == 0:
                fbuf[...] = part
            else:
                fbuf[...] = fbuf[...] + part

    last = [0]
    for s in range(1, half + 1):
        now = []
        for h in (0, 1):
            for way, todo in (("gup", gup), ("gdown", gdown)):
                if (s, h) in todo:
                    gring_recv(way, s, h).wait_recv()
                    if (s + 1, h) in todo:
                        begin(gring(way, s + 1, h))
                    o = -s if way == "gup" else s
                    if s == half:
                        o = half
                    begin(gpair(o, h))
                    if o not in now:
                        now.append(o)
        for o in last:
            feature(o)
        last = now
    for o in last:
        feature(o)

    def fa_copy(j):
        p = lax.rem(tok + j, nt)
        return rcopy(fbuf.at[p], fabuf.at[tok], "fa", j, {"tok": p})

    def fr_copy(j):
        p = lax.rem(voc + j, nv)
        return rcopy(fabuf.at[pl.ds(p * spv, spv)], frbuf.at[voc], "fr", j, {"vocab": p})

    def fb_copy(j, other):
        p = lax.rem(voc + j, nv)
        return rcopy(fbb.at[voc], fbb.at[voc], "fb", other * nv + j, {"mp": other, "vocab": p})

    @pl.when(mp == 0)
    def _():
        @pl.loop(1, nt)
        def _(j):
            fa_copy(j).start()

        fabuf[tok] = fbuf[tok]

    for c in (dw_copy, unit_copy, inv_copy):
        c.wait_recv()
    dw = jnp.where(mp == 0, colb[...].astype(f32), dwb[...].astype(f32)).astype(bf16)

    def hcopy(i):
        return pltpu.make_async_copy(hbuf.at[i], head_out.at[0, pl.ds(i * chip_rows, chip_rows), :], hsem.at[i])

    def head_rows(i):
        z = mp * half + i
        hbuf[i, 0:R, :] = jnp.dot(gbuf[0, z], dw, preferred_element_type=f32).astype(bf16)
        hbuf[i, R:chip_rows, :] = jnp.dot(
            gbuf[1, z, over:R, :], dw, preferred_element_type=f32).astype(bf16)
        hcopy(i).start()

    for i in range(half // 2):
        head_rows(i)

    @pl.when(mp == 0)
    def _():
        @pl.loop(1, nt)
        def _(j):
            fa_copy(j).wait_recv()

        @pl.loop(1, nv)
        def _(j):
            fr_copy(j).start()

        frbuf[voc] = fabuf[pl.ds(voc * spv, spv)]

    for i in range(half // 2, half):
        head_rows(i)

    @pl.when(mp == 0)
    def _():
        @pl.loop(1, nv)
        def _(j):
            fr_copy(j).wait_recv()

        scaled = jnp.sum(frbuf[...], axis=0) * gainb[pl.ds(voc * spv, spv)]
        mine = ubuf[pl.ds(voc * spv, spv)] * scaled
        dot = jnp.sum(jnp.sum(mine, axis=2, keepdims=True), axis=0)
        fbb[voc, 0:spv] = scaled
        fbb[voc, spv] = jnp.broadcast_to(dot, (8, width))

        @pl.loop(1, nv)
        def _(j):
            fb_copy(j, 0).start()

        @pl.loop(0, nv)
        def _(j):
            fb_copy(j, 1).start()

        @pl.loop(1, nv)
        def _(j):
            fb_copy(j, 0).wait_recv()

    @pl.when(mp == 1)
    def _():
        @pl.loop(0, nv)
        def _(j):
            fb_copy(j, 1).wait_recv()

    mean = jnp.sum(fbb[:, spv], axis=0) * (1.0 / (nt * width))
    inv_pol = jnp.where(mp == 0, ibuf[:, 0:1], irecv[:, 0:1])
    for i in range(nt // 2):
        slab = mp * (nt // 2) + i
        unit_pol = jnp.where(mp == 0, ubuf[i], urecv[i])
        hg_out[i] = inv_pol * (fbb[slab // spv, lax.rem(slab, spv)] - unit_pol * mean)

    for i in range(half):
        hcopy(i).wait()
    for c in pending:
        c.wait_send()

    @pl.loop(1, nt)
    def _(j):
        a2a_copy(j).wait_send()
        meta_copy(j).wait_send()
        tstat_copy(j).wait_send()

    @pl.loop(1, nv)
    def _(j):
        vstat_copy(j).wait_send()

    @pl.when(mp == 0)
    def _():
        @pl.loop(1, nt)
        def _(j):
            fa_copy(j).wait_send()

        @pl.loop(1, nv)
        def _(j):
            fr_copy(j).wait_send()
            fb_copy(j, 0).wait_send()

        @pl.loop(0, nv)
        def _(j):
            fb_copy(j, 1).wait_send()


def per_device(nt, nv, hidden, norm_gain, output_head, token_ids, live_mask, advantages):
    nz = nt // 2
    half = nz // 2
    rows, width = output_head.shape[1:]
    chip_rows = rows // nz
    R = (chip_rows // 2 + 31) // 32 * 32
    T = nt * 8
    spv = nt // nv
    ring = 2 + 4 * (half - 1)
    plan, n_sem = sem_plan(nt, nz, nv)
    vmem = pl.BlockSpec(memory_space=pltpu.VMEM)
    smem = pl.BlockSpec(memory_space=pltpu.SMEM)
    hbm = pl.BlockSpec(memory_space=pl.ANY)
    V = pltpu.VMEM
    hg, head_part = pl.pallas_call(
        functools.partial(kernel, nt, nz, nv, plan, n_sem),
        out_shape=(
            jax.ShapeDtypeStruct((nt // 2, 8, width), f32),
            jax.ShapeDtypeStruct((1, rows // 2, width), bf16),
        ),
        in_specs=[vmem, vmem, hbm, smem, smem, smem],
        out_specs=(vmem, hbm),
        scratch_shapes=[
            V((nz, chip_rows, width), bf16),
            V((nz, chip_rows, T), f32),
            V((nz, R, T), f32),
            V((2 * ring, R // 4, T), f32),
            V((R, T), f32),
            V((2, nz, R, T), bf16),
            V((half, chip_rows, width), bf16),
            V((nt, 8, width), f32),
            V((nt, 8, width), f32),
            V((nt, 8, width), f32),
            V((nt // 2, 8, width), f32),
            V((8, 128), f32),
            V((8, 128), f32),
            V((nt, 8, width), f32),
            V((nt, 8, T), f32),
            V((T, width), bf16),
            V((T, width), bf16),
            V((nt, 8, T), f32),
            V((nv, 8, T), f32),
            V((nt, 8, width), f32),
            V((nt, 8, width), f32),
            V((nv, spv, 8, width), f32),
            V((nv, spv + 1, 8, width), f32),
            pltpu.SemaphoreType.DMA((nz,)),
            pltpu.SemaphoreType.DMA((half,)),
            pltpu.SemaphoreType.DMA((n_sem,)),
            pltpu.SemaphoreType.DMA((n_sem,)),
        ],
        compiler_params=pltpu.CompilerParams(
            collective_id=0, has_side_effects=True, vmem_limit_bytes=56 * 2**20),
        cost_estimate=pl.CostEstimate(
            flops=5 * rows * width * T, bytes_accessed=3 * rows * width, transcendentals=3 * R * T),
    )(hidden, norm_gain, output_head, token_ids, live_mask, advantages)
    return hg.transpose(1, 0, 2).reshape(8, nt // 2 * width), head_part


def solution(mesh):
    placed = (
        P("mp", "tok", None),
        P("mp", None),
        P("mp", "vocab", "tok"),
        P("tok"),
        P("tok"),
        P("tok"),
    )
    return jax.shard_map(
        functools.partial(per_device, mesh.shape["tok"], mesh.shape["vocab"]),
        mesh=mesh,
        in_specs=placed,
        out_specs=(P("tok", "mp"), P("mp", "vocab", "tok")),
        check_vma=False,
    )
```

```python
import functools

import jax
import jax.numpy as jnp
from jax import lax
from jax.experimental import pallas as pl
from jax.experimental.pallas import tpu as pltpu
from jax.sharding import PartitionSpec as P

loss_scale = 256.0
kl_coef = 0.1
norm_eps = 1e-06
MESH = pl.DeviceIdType.MESH
f32 = jnp.float32
bf16 = jnp.bfloat16
LANES = 128


def pieces_of(blocks, number):
    sizes = [(blocks + number - 1 - i) // number for i in range(number)]
    starts = [sum(sizes[:i]) for i in range(number)]
    return [(a * LANES, n * LANES) for a, n in zip(starts, sizes)]


RING = 8
GATHER = 4


def sem_plan(nt, nz, nv):
    sizes = dict(
        a2a=nt, meta=nt, dw=1, unit=1, inv=1, pair=RING, up=RING * nz, down=RING * nz, peer=RING, stat=2 * nv,
        gup=GATHER * nz, gdown=GATHER * nz, gpair=GATHER * nz, fa=nt, fr=nv, fb=nv, fm=2 * nv)
    plan, count = {}, 0
    for name, size in sizes.items():
        plan[name] = count
        count += size
    return plan, count


def kernel(nt, nz, nv, plan,
           hidden, gain, head, ids, live, adv,
           hg_out, head_out,
           wbuf, lsib, lown, xbuf, rbuf, ybuf, gbuf, hbuf,
           nbuf, cbuf, ubuf, urecv, ibuf, irecv, gainb, mbuf, colb, dwb,
           stat, fbuf, fabuf, frbuf, fbb, dots,
           wsem, hsem, ss, rs):
    mp = lax.axis_index("mp")
    tok = lax.axis_index("tok")
    voc = lax.axis_index("vocab")
    zi = tok // 2
    core = tok % 2
    sib = tok + 1 - 2 * core
    half = nz // 2
    T = nt * 8
    width, vocab_dev = wbuf.shape
    kh = width // 2
    W = xbuf.shape[1]
    off = vocab_dev - W
    over = W - off
    spv = nt // nv
    rpieces = pieces_of(W // LANES, RING)
    gpieces = pieces_of(W // LANES, GATHER)
    pending = []

    def rcopy(src, dst, name, index, dev):
        at = plan[name] + index
        return pltpu.make_async_remote_copy(
            src_ref=src, dst_ref=dst, send_sem=ss.at[at], recv_sem=rs.at[at],
            device_id=dev, device_id_type=MESH)

    def begin(c):
        c.start()
        pending.append(c)

    def zat(o):
        return lax.rem(zi + o + nz, nz)

    def rows_of(o):
        return pl.ds(pl.multiple_of(zat(o) * 16, 16), 16)

    def way_dev(way):
        return {"tok": lax.rem(tok + (2 if way == "up" else nt - 2), nt)}

    def wcopy(k):
        return pltpu.make_async_copy(
            head.at[0, pl.ds(k * kh, kh), :], wbuf.at[pl.ds(k * kh, kh), :], wsem.at[k])

    for k in range(2):
        wcopy(k).start()

    barrier = pltpu.get_barrier_semaphore()

    def greet(dev):
        pl.semaphore_signal(barrier, inc=1, device_id=dev, device_id_type=MESH)

    @pl.loop(1, nt)
    def _(j):
        greet({"tok": lax.rem(tok + j, nt)})

    @pl.loop(1, nv)
    def _(j):
        greet({"vocab": lax.rem(voc + j, nv)})
        greet({"tok": sib, "vocab": lax.rem(voc + j, nv)})

    @pl.loop(0, nv)
    def _(j):
        greet({"mp": 1 - mp, "vocab": lax.rem(voc + j, nv)})

    x = hidden[0].astype(f32)
    inv = lax.rsqrt(jnp.mean(x * x, axis=1, keepdims=True) + norm_eps)
    unit = x * inv
    g = gain[...]
    normed = unit * g
    for k in range(nt):
        a = k * width
        nbuf[k] = jnp.concatenate(
            [normed[:, a:a + kh], normed[:, a + kh:a + width]], axis=0).astype(bf16)
    cbuf[tok] = nbuf[tok]

    pl.semaphore_wait(barrier, nt - 1 + 2 * (nv - 1) + nv)

    def a2a_copy(j):
        p = lax.rem(tok + j, nt)
        return rcopy(nbuf.at[p], cbuf.at[tok], "a2a", j, {"tok": p})

    def meta_copy(j):
        p = lax.rem(tok + j, nt)
        return rcopy(mbuf.at[tok], mbuf.at[tok], "meta", j, {"tok": p})

    @pl.loop(1, nt)
    def _(j):
        a2a_copy(j).start()

    for k in range(nt):
        cols = slice(k * width, (k + 1) * width)
        ubuf[k] = unit[:, cols]
        gainb[k] = jnp.broadcast_to(g[:, cols], (8, width))
    ibuf[...] = jnp.broadcast_to(inv, ibuf.shape)
    lane = lax.broadcasted_iota(jnp.int32, (8, LANES), 1)
    row = lax.broadcasted_iota(jnp.int32, (8, LANES), 0)
    info = jnp.zeros((8, LANES), f32)
    for j in range(8):
        mine = jnp.where(lane == 0, ids[j].astype(f32), jnp.where(lane == 1, live[j].astype(f32), adv[j]))
        info = jnp.where(row == j, mine, info)
    mbuf[tok] = info
    for k in range(2):
        wcopy(k).wait()

    @pl.loop(1, nt)
    def _(j):
        a2a_copy(j).wait_recv()

    cols = cbuf[...].astype(f32)
    colb[0] = cols[:, 0:8, :].reshape(T, kh).astype(bf16)
    colb[1] = cols[:, 8:16, :].reshape(T, kh).astype(bf16)

    def dot_piece(window, q):
        a, n = rpieces[q]
        at = pl.ds(pl.multiple_of(window * off + a, LANES), n)
        return jnp.dot(colb[0], wbuf[0:kh, at], preferred_element_type=f32) + jnp.dot(
            colb[1], wbuf[kh:width, at], preferred_element_type=f32)

    def lanes(q):
        a, n = rpieces[q]
        return pl.ds(a, n)

    def glanes(q):
        a, n = gpieces[q]
        return pl.ds(a, n)

    def pair_copy(q):
        return rcopy(lsib.at[:, lanes(q)], xbuf.at[:, lanes(q)], "pair", q, {"tok": sib})

    def logits(q):
        lsib[:, lanes(q)] = dot_piece(1 - core, q)
        begin(pair_copy(q))
        lown[:, lanes(q)] = dot_piece(core, q)

    def chain(way, q):
        first = half if (way == "up") == (q % 2 == 0) else half - 1
        return list(range(first, 0, -1))

    def ring_copy(way, d, q):
        o = d if way == "up" else -d
        w = 0 if way == "up" else 1
        return rcopy(
            xbuf.at[rows_of(o), lanes(q)], rbuf.at[w, d - 1, :, lanes(q)], way, (d - 1) * RING + q, way_dev(way))

    done = {}

    def peer_copy(q):
        return rcopy(xbuf.at[rows_of(0), lanes(q)], ybuf.at[:, lanes(q)], "peer", q, {"mp": 1 - mp})

    def logits_ready(q):
        pair_copy(q).wait_recv()
        xbuf[:, lanes(q)] = xbuf[:, lanes(q)] + lown[:, lanes(q)]
        for way in ("up", "down"):
            begin(ring_copy(way, chain(way, q)[0], q))
        done[q] = 0

    def step(way, q, hop):
        ds = chain(way, q)
        if hop > len(ds):
            return
        d = ds[hop - 1]
        ring_copy(way, d, q).wait_recv()
        o = d - 1 if way == "up" else 1 - d
        w = 0 if way == "up" else 1
        xbuf[rows_of(o), lanes(q)] = xbuf[rows_of(o), lanes(q)] + rbuf[w, d - 1, :, lanes(q)]
        if d > 1:
            begin(ring_copy(way, d - 1, q))
            return
        done[q] += 1
        if done[q] == 2:
            begin(peer_copy(q))

    dw_copy = rcopy(colb, dwb, "dw", 0, {"mp": 1 - mp})
    unit_copy = rcopy(ubuf.at[pl.ds(nt // 2, nt // 2)], urecv, "unit", 0, {"mp": 1 - mp})
    inv_copy = rcopy(ibuf, irecv, "inv", 0, {"mp": 1 - mp})

    def steps(hop, q):
        step("up", q, hop)
        step("down", q, hop)

    lead = 3 * RING // 4
    for q in range(RING):
        logits(q)
        if q == 0:
            for c in (dw_copy, unit_copy, inv_copy):
                begin(c)
        else:
            logits_ready(q - 1)
        if q >= lead:
            steps(1, q - lead)
    logits_ready(RING - 1)

    @pl.loop(1, nt)
    def _(j):
        meta_copy(j).start()

    for hop in range(1, half + 1):
        for q in range(RING):
            if hop > 1 or q >= RING - lead:
                steps(hop, q)

    for q in range(RING):
        peer_copy(q).wait_recv()

    own = xbuf[rows_of(0), :]
    peer = ybuf[...]
    l0 = jnp.where(mp == 0, own, peer)
    l1 = jnp.where(mp == 0, peer, own)
    lid = lax.broadcasted_iota(jnp.int32, (1, W), 1)
    counted = jnp.where((lid >= over) | (core == 0), 1.0, 0.0).astype(f32)
    lane16 = lax.broadcasted_iota(jnp.int32, (16, LANES), 1)

    def in_lanes(a, b, c):
        return jnp.where(lane16 == 0, a, jnp.where(lane16 == 1, b, c))

    h0 = jnp.max(l0, axis=1, keepdims=True)
    h1 = jnp.max(l1, axis=1, keepdims=True)
    e0 = jnp.exp(l0 - h0) * counted
    e1 = jnp.exp(l1 - h1) * counted
    me = core * nv + voc
    stat[me, 0] = in_lanes(h0, h0, h1)
    stat[me, 1] = in_lanes(
        jnp.sum(e0, axis=1, keepdims=True), jnp.sum(e0 * (l0 - l1), axis=1, keepdims=True),
        jnp.sum(e1, axis=1, keepdims=True))

    def stat_copy(other, j):
        dev = {"tok": sib if other else tok, "vocab": lax.rem(voc + j, nv)}
        return rcopy(stat.at[me], stat.at[me], "stat", other * nv + j, dev)

    @pl.loop(1, nv)
    def _(j):
        stat_copy(0, j).start()
        stat_copy(1, j).start()

    stat_copy(1, 0).start()

    @pl.loop(1, nt)
    def _(j):
        meta_copy(j).wait_recv()

    live_total = jnp.sum(jnp.sum(mbuf[...], axis=0), axis=0, keepdims=True)[:, 1:2]
    infos = mbuf[pl.ds(2 * zi, 2)].reshape(16, LANES)
    id_col = infos[:, 0:1].astype(jnp.int32)
    coef = loss_scale * infos[:, 1:2] / live_total
    adv_col = infos[:, 2:3]
    entry = voc * vocab_dev + core * off + lid
    onehot = jnp.where(entry == id_col, 1.0, 0.0).astype(f32)

    stat_copy(1, 0).wait_recv()

    @pl.loop(1, nv)
    def _(j):
        stat_copy(0, j).wait_recv()
        stat_copy(1, j).wait_recv()

    highs = stat[:, 0]
    high = jnp.max(highs, axis=0)
    total = jnp.sum(stat[:, 1] * jnp.exp(highs - high[None]), axis=0)
    log_total = jnp.log(total)
    lse0 = high[:, 0:1] + log_total[:, 0:1]
    lse1 = high[:, 2:3] + log_total[:, 2:3]
    kl = total[:, 1:2] / total[:, 0:1] - (lse0 - lse1)

    lp0 = l0 - lse0
    diff = lp0 - (l1 - lse1)
    prob = jnp.exp(lp0)
    gbuf[core, rows_of(0), :] = (
        coef * (adv_col * (prob - onehot) + kl_coef * prob * (diff - kl))).astype(bf16)

    def gchain(way, q):
        return half if (way == "up") == (q % 2 == 0) else half - 1

    def gring(way, s, q, arriving=False):
        back = s if arriving else s - 1
        view = gbuf.at[core, rows_of(-back if way == "up" else back), glanes(q)]
        return rcopy(view, view, "g" + way, (s - 1) * GATHER + q, way_dev(way))

    def gpair(o, q, arriving=False):
        view = gbuf.at[1 - core if arriving else core, rows_of(o), glanes(q)]
        return rcopy(view, view, "gpair", (o % nz) * GATHER + q, {"tok": sib})

    for q in range(GATHER):
        for way in ("up", "down"):
            if gchain(way, q) >= 1:
                begin(gring(way, 1, q))
        begin(gpair(0, q))

    def gstep(s, qs):
        for q in qs:
            for way in ("up", "down"):
                if s > gchain(way, q):
                    continue
                gring(way, s, q, True).wait_recv()
                if s < gchain(way, q):
                    begin(gring(way, s + 1, q))
                begin(gpair(-s if way == "up" else s, q))

    def gather_end(q):
        for o in range(nz):
            gpair(o, q, True).wait_recv()

    def feature(q):
        @pl.when(mp == 0)
        def _():
            a, n = gpieces[q]
            nt_dims = (((1,), (1,)), ((), ()))
            skip = over if q == 0 else 0
            part = lax.dot_general(
                gbuf[0, :, a:a + n], wbuf[:, a:a + n], nt_dims, preferred_element_type=f32)
            part = part + lax.dot_general(
                gbuf[1, :, a + skip:a + n], wbuf[:, off + a + skip:off + a + n], nt_dims,
                preferred_element_type=f32)
            part = part.reshape(nt, 8, width)
            if q == 0:
                fbuf[...] = part
            else:
                fbuf[...] = fbuf[...] + part

    every = range(GATHER)
    for s in range(1, half):
        gstep(s, every)
    gstep(half, (0,))
    for q in every:
        if q + 1 < GATHER:
            gstep(half, (q + 1,))
        gather_end(q)
        feature(q)

    def fa_copy(j):
        p = lax.rem(tok + j, nt)
        return rcopy(fbuf.at[p], fabuf.at[tok], "fa", j, {"tok": p})

    def fr_copy(j):
        p = lax.rem(voc + j, nv)
        return rcopy(fabuf.at[pl.ds(p * spv, spv)], frbuf.at[voc], "fr", j, {"vocab": p})

    target = voc // (nv // 2)

    def fb_copy(j):
        p = lax.rem(voc + j, nv)
        return rcopy(fbb.at[voc], fbb.at[voc], "fb", j, {"mp": target, "vocab": p})

    def fm_copy(j, other):
        p = lax.rem(voc + j, nv)
        return rcopy(dots.at[voc], dots.at[voc], "fm", other * nv + j, {"mp": other, "vocab": p})

    def due(j):
        return lax.rem(voc - j + nv, nv) // (nv // 2) == mp

    @pl.when(mp == 0)
    def _():
        @pl.loop(1, nt)
        def _(j):
            fa_copy(j).start()

        fabuf[tok] = fbuf[tok]

    for c in (dw_copy, unit_copy, inv_copy):
        c.wait_recv()
    n_half = vocab_dev // 2
    shift = n_half - off

    def hcopy(k):
        return pltpu.make_async_copy(
            hbuf.at[pl.ds(k * kh, kh), :], head_out.at[0, pl.ds(k * kh, kh), :], hsem.at[k])

    def head_rows(k):
        dw = jnp.where(mp == 0, colb[k].astype(f32), dwb[k].astype(f32)).T.astype(bf16)
        for a, n in gpieces:
            n = min(n, n_half - a)

            @pl.when(mp == 0)
            def _():
                hbuf[k * kh:(k + 1) * kh, a:a + n] = jnp.dot(
                    dw, gbuf[0, :, a:a + n], preferred_element_type=f32).astype(bf16)

            @pl.when(mp == 1)
            def _():
                wide = min(n + LANES, W - a)
                hbuf[k * kh:(k + 1) * kh, a:a + n] = jnp.dot(
                    dw, gbuf[1, :, a:a + wide][:, shift:shift + n], preferred_element_type=f32).astype(bf16)
        hcopy(k).start()

    head_rows(0)

    @pl.when(mp == 0)
    def _():
        @pl.loop(1, nt)
        def _(j):
            fa_copy(j).wait_recv()

        @pl.loop(1, nv)
        def _(j):
            fr_copy(j).start()

        frbuf[voc] = fabuf[pl.ds(voc * spv, spv)]

    head_rows(1)

    @pl.when(mp == 0)
    def _():
        @pl.loop(1, nv)
        def _(j):
            fr_copy(j).wait_recv()

        scaled = jnp.sum(frbuf[...], axis=0) * gainb[pl.ds(voc * spv, spv)]
        mine = ubuf[pl.ds(voc * spv, spv)] * scaled
        dot = jnp.sum(jnp.sum(mine, axis=2, keepdims=True), axis=0)
        fbb[voc] = scaled
        dots[voc] = jnp.broadcast_to(dot, (8, LANES))

        @pl.loop(1, nv)
        def _(j):
            fb_copy(j).start()
            fm_copy(j, 0).start()
            fm_copy(j, 1).start()

        fm_copy(0, 1).start()

        @pl.when(target == 1)
        def _():
            fb_copy(0).start()

        @pl.loop(1, nv)
        def _(j):
            fm_copy(j, 0).wait_recv()

            @pl.when(due(j))
            def _():
                fb_copy(j).wait_recv()

    @pl.when(mp == 1)
    def _():
        @pl.loop(0, nv)
        def _(j):
            fm_copy(j, 1).wait_recv()

            @pl.when(due(j))
            def _():
                fb_copy(j).wait_recv()

    mean = jnp.sum(dots[...], axis=0)[:, 0:1] * (1.0 / (nt * width))
    inv_pol = jnp.where(mp == 0, ibuf[:, 0:1], irecv[:, 0:1])
    for i in range(nt // 2):
        slab = mp * (nt // 2) + i
        unit_pol = jnp.where(mp == 0, ubuf[i], urecv[i])
        hg_out[:, i * width:(i + 1) * width] = inv_pol * (
            fbb[slab // spv, lax.rem(slab, spv)] - unit_pol * mean)

    for k in range(2):
        hcopy(k).wait()
    for c in pending:
        c.wait_send()

    @pl.loop(1, nt)
    def _(j):
        a2a_copy(j).wait_send()
        meta_copy(j).wait_send()

    stat_copy(1, 0).wait_send()

    @pl.loop(1, nv)
    def _(j):
        stat_copy(0, j).wait_send()
        stat_copy(1, j).wait_send()

    @pl.when(mp == 0)
    def _():
        @pl.loop(1, nt)
        def _(j):
            fa_copy(j).wait_send()

        @pl.loop(1, nv)
        def _(j):
            fr_copy(j).wait_send()
            fb_copy(j).wait_send()
            fm_copy(j, 0).wait_send()
            fm_copy(j, 1).wait_send()

        fm_copy(0, 1).wait_send()

        @pl.when(target == 1)
        def _():
            fb_copy(0).wait_send()


def per_device(nt, nv, hidden, norm_gain, output_head, token_ids, live_mask, advantages):
    nz = nt // 2
    half = nz // 2
    rows, width = output_head.shape[1:]
    kh = width // 2
    blocks = rows // LANES
    W = (blocks + 1) // 2 * LANES
    T = nt * 8
    spv = nt // nv
    plan, n_sem = sem_plan(nt, nz, nv)
    vmem = pl.BlockSpec(memory_space=pltpu.VMEM)
    smem = pl.BlockSpec(memory_space=pltpu.SMEM)
    hbm = pl.BlockSpec(memory_space=pl.ANY)
    V = pltpu.VMEM
    hg, head_part = pl.pallas_call(
        functools.partial(kernel, nt, nz, nv, plan),
        out_shape=(
            jax.ShapeDtypeStruct((8, nt // 2 * width), f32),
            jax.ShapeDtypeStruct((1, width, rows // 2), bf16),
        ),
        in_specs=[vmem, vmem, hbm, smem, smem, smem],
        out_specs=(vmem, hbm),
        scratch_shapes=[
            V((width, rows), bf16),
            V((T, W), f32),
            V((T, W), f32),
            V((T, W), f32),
            V((2, half, 16, W), f32),
            V((16, W), f32),
            V((2, T, W), bf16),
            V((width, rows // 2), bf16),
            V((nt, 16, kh), bf16),
            V((nt, 16, kh), bf16),
            V((nt, 8, width), f32),
            V((nt // 2, 8, width), f32),
            V((8, LANES), f32),
            V((8, LANES), f32),
            V((nt, 8, width), f32),
            V((nt, 8, LANES), f32),
            V((2, T, kh), bf16),
            V((2, T, kh), bf16),
            V((2 * nv, 2, 16, LANES), f32),
            V((nt, 8, width), f32),
            V((nt, 8, width), f32),
            V((nv, spv, 8, width), f32),
            V((nv, spv, 8, width), f32),
            V((nv, 8, LANES), f32),
            pltpu.SemaphoreType.DMA((2,)),
            pltpu.SemaphoreType.DMA((2,)),
            pltpu.SemaphoreType.DMA((n_sem,)),
            pltpu.SemaphoreType.DMA((n_sem,)),
        ],
        compiler_params=pltpu.CompilerParams(
            collective_id=0, has_side_effects=True, vmem_limit_bytes=56 * 2**20),
        cost_estimate=pl.CostEstimate(
            flops=5 * rows * width * T, bytes_accessed=3 * rows * width, transcendentals=3 * 16 * W),
    )(hidden, norm_gain, jnp.swapaxes(output_head, 1, 2), token_ids, live_mask, advantages)
    return hg, jnp.swapaxes(head_part, 1, 2)


def solution(mesh):
    placed = (
        P("mp", "tok", None),
        P("mp", None),
        P("mp", "vocab", "tok"),
        P("tok"),
        P("tok"),
        P("tok"),
    )
    return jax.shard_map(
        functools.partial(per_device, mesh.shape["tok"], mesh.shape["vocab"]),
        mesh=mesh,
        in_specs=placed,
        out_specs=(P("tok", "mp"), P("mp", "vocab", "tok")),
        check_vma=False,
    )
```

```python
import functools

import jax
import jax.numpy as jnp
from jax import lax
from jax.experimental import pallas as pl
from jax.experimental.pallas import tpu as pltpu
from jax.sharding import PartitionSpec as P

loss_scale = 256.0
kl_coef = 0.1
norm_eps = 1e-06
MESH = pl.DeviceIdType.MESH
f32 = jnp.float32
bf16 = jnp.bfloat16
LANES = 128


def pieces_of(blocks, number):
    sizes = [(blocks + number - 1 - i) // number for i in range(number)]
    starts = [sum(sizes[:i]) for i in range(number)]
    return [(a * LANES, n * LANES) for a, n in zip(starts, sizes)]


RING = 8
TURNS = 2
HEAD_PARTS = 4


def sem_plan(nt, nz, nv):
    sizes = dict(
        a2a=nt, meta=nt, dw=1, unit=1, inv=1, pair=RING, up=RING * nz, down=RING * nz, peer=RING, stat=2 * nv, gs=2 * TURNS * nz,
        gz=TURNS * nz, gx=TURNS * nz, gxs=TURNS * nz, fa=nt, fr=nv, fb=nv, fm=2 * nv)
    plan, count = {}, 0
    for name, size in sizes.items():
        plan[name] = count
        count += size
    return plan, count


def kernel(nt, nz, nv, plan,
           hidden, gain, head, ids, live, adv,
           hg_out, head_out,
           wbuf, lsib, lown, xbuf, rbuf, ybuf, gbuf, hbuf,
           nbuf, cbuf, ubuf, urecv, ibuf, irecv, gainb, mbuf, colb, dwb,
           stat, fbuf, fabuf, frbuf, fbb, dots,
           wsem, hsem, ss, rs):
    mp = lax.axis_index("mp")
    tok = lax.axis_index("tok")
    voc = lax.axis_index("vocab")
    zi = tok // 2
    core = tok % 2
    sib = tok + 1 - 2 * core
    half = nz // 2
    T = nt * 8
    width, vocab_dev = wbuf.shape
    kh = width // 2
    W = gbuf.shape[2]
    off = vocab_dev - W
    over = W - off
    spv = nt // nv
    rpieces = pieces_of(W // LANES, RING)
    turns = pieces_of(W // LANES // 2, TURNS)
    hpieces = pieces_of(W // LANES, HEAD_PARTS)
    active = mp == core
    held = {}
    pending = []

    def rcopy(src, dst, name, index, dev):
        at = plan[name] + index
        return pltpu.make_async_remote_copy(
            src_ref=src, dst_ref=dst, send_sem=ss.at[at], recv_sem=rs.at[at],
            device_id=dev, device_id_type=MESH)

    def begin(c):
        c.start()
        pending.append(c)

    def begin_if(when, make, *at):
        make(*at).start()
        held.setdefault(when, []).append((make, at))

    def zat(o):
        return lax.rem(zi + o + nz, nz)

    def rows_of(o):
        return pl.ds(pl.multiple_of(zat(o) * 16, 16), 16)

    def way_dev(way):
        return {"tok": lax.rem(tok + (2 if way == "up" else nt - 2), nt)}

    def wcopy(k):
        return pltpu.make_async_copy(
            head.at[0, pl.ds(k * kh, kh), :], wbuf.at[pl.ds(k * kh, kh), :], wsem.at[k])

    for k in range(2):
        wcopy(k).start()

    barrier = pltpu.get_barrier_semaphore()

    def greet(dev):
        pl.semaphore_signal(barrier, inc=1, device_id=dev, device_id_type=MESH)

    @pl.loop(1, nt)
    def _(j):
        greet({"tok": lax.rem(tok + j, nt)})

    @pl.loop(1, nv)
    def _(j):
        greet({"vocab": lax.rem(voc + j, nv)})

    @pl.loop(0, nv)
    def _(j):
        greet({"mp": 1 - mp, "vocab": lax.rem(voc + j, nv)})
        greet({"mp": 1 - mp, "tok": sib, "vocab": lax.rem(voc + j, nv)})

    x = hidden[0].astype(f32)
    inv = lax.rsqrt(jnp.mean(x * x, axis=1, keepdims=True) + norm_eps)
    unit = x * inv
    g = gain[...]
    normed = unit * g
    for k in range(nt):
        a = k * width
        nbuf[k] = jnp.concatenate(
            [normed[:, a:a + kh], normed[:, a + kh:a + width]], axis=0).astype(bf16)
    cbuf[tok] = nbuf[tok]

    pl.semaphore_wait(barrier, nt - 1 + nv - 1 + 2 * nv)

    def a2a_copy(j):
        p = lax.rem(tok + j, nt)
        return rcopy(nbuf.at[p], cbuf.at[tok], "a2a", j, {"tok": p})

    def meta_copy(j):
        p = lax.rem(tok + j, nt)
        return rcopy(mbuf.at[tok], mbuf.at[tok], "meta", j, {"tok": p})

    @pl.loop(1, nt)
    def _(j):
        a2a_copy(j).start()

    for k in range(nt):
        cols = slice(k * width, (k + 1) * width)
        ubuf[k] = unit[:, cols]
        gainb[k] = jnp.broadcast_to(g[:, cols], (8, width))
    ibuf[...] = jnp.broadcast_to(inv, ibuf.shape)
    lane = lax.broadcasted_iota(jnp.int32, (8, LANES), 1)
    row = lax.broadcasted_iota(jnp.int32, (8, LANES), 0)
    info = jnp.zeros((8, LANES), f32)
    for j in range(8):
        mine = jnp.where(lane == 0, ids[j].astype(f32), jnp.where(lane == 1, live[j].astype(f32), adv[j]))
        info = jnp.where(row == j, mine, info)
    mbuf[tok] = info
    for k in range(2):
        wcopy(k).wait()

    @pl.loop(1, nt)
    def _(j):
        a2a_copy(j).wait_recv()

    cols = cbuf[...].astype(f32)
    colb[0] = cols[:, 0:8, :].reshape(T, kh).astype(bf16)
    colb[1] = cols[:, 8:16, :].reshape(T, kh).astype(bf16)

    def dot_piece(window, q):
        a, n = rpieces[q]
        at = pl.ds(pl.multiple_of(window * off + a, LANES), n)
        return jnp.dot(colb[0], wbuf[0:kh, at], preferred_element_type=f32) + jnp.dot(
            colb[1], wbuf[kh:width, at], preferred_element_type=f32)

    def lanes(q):
        return pl.ds(0, rpieces[q][1])

    def glanes(i, who):
        a, n = turns[i]
        return pl.ds(pl.multiple_of(2 * a + who * n, LANES), n)

    def pair_copy(q):
        return rcopy(lsib.at[q, :, lanes(q)], xbuf.at[q, :, lanes(q)], "pair", q, {"tok": sib})

    def logits(q):
        lsib[q, :, lanes(q)] = dot_piece(1 - core, q)
        begin(pair_copy(q))
        lown[q, :, lanes(q)] = dot_piece(core, q)

    def chain(way, q):
        first = half if (way == "up") == (q % 2 == 0) else half - 1
        return list(range(first, 0, -1))

    def ring_copy(way, d, q):
        o = d if way == "up" else -d
        w = 0 if way == "up" else 1
        return rcopy(
            xbuf.at[q, rows_of(o), lanes(q)], rbuf.at[w, d - 1, q, :, lanes(q)], way, (d - 1) * RING + q, way_dev(way))

    done = {}

    def peer_copy(q):
        return rcopy(xbuf.at[q, rows_of(0), lanes(q)], ybuf.at[q, :, lanes(q)], "peer", q, {"mp": 1 - mp})

    def logits_ready(q):
        pair_copy(q).wait_recv()
        xbuf[q, :, lanes(q)] = xbuf[q, :, lanes(q)] + lown[q, :, lanes(q)]
        for way in ("up", "down"):
            begin(ring_copy(way, chain(way, q)[0], q))
        done[q] = 0

    def step(way, q, hop):
        ds = chain(way, q)
        if hop > len(ds):
            return
        d = ds[hop - 1]
        ring_copy(way, d, q).wait_recv()
        o = d - 1 if way == "up" else 1 - d
        w = 0 if way == "up" else 1
        xbuf[q, rows_of(o), lanes(q)] = xbuf[q, rows_of(o), lanes(q)] + rbuf[w, d - 1, q, :, lanes(q)]
        if d > 1:
            begin(ring_copy(way, d - 1, q))
            return
        done[q] += 1
        if done[q] == 2:
            @pl.when(jnp.logical_not(active))
            def _():
                begin_if("idle", peer_copy, q)

    dw_copy = rcopy(colb, dwb, "dw", 0, {"mp": 1 - mp})
    unit_copy = rcopy(ubuf.at[pl.ds(nt // 2, nt // 2)], urecv, "unit", 0, {"mp": 1 - mp})
    inv_copy = rcopy(ibuf, irecv, "inv", 0, {"mp": 1 - mp})

    def steps(hop, q):
        step("up", q, hop)
        step("down", q, hop)

    lead = 3 * RING // 4
    for q in range(RING):
        logits(q)
        if q == 0:
            for c in (dw_copy, unit_copy, inv_copy):
                begin(c)
        else:
            logits_ready(q - 1)
        if q >= lead:
            steps(1, q - lead)
    logits_ready(RING - 1)

    @pl.loop(1, nt)
    def _(j):
        meta_copy(j).start()

    for hop in range(1, half + 1):
        for q in range(RING):
            if hop > 1 or q >= RING - lead:
                steps(hop, q)

    @pl.loop(1, nt)
    def _(j):
        meta_copy(j).wait_recv()

    me = mp * nv + voc

    def stat_copy(other, j):
        dev = {"vocab": lax.rem(voc + j, nv)}
        if other:
            dev.update({"mp": 1 - mp, "tok": sib})
        return rcopy(stat.at[me], stat.at[me], "stat", other * nv + j, dev)

    def gs_copy(o, i, who):
        view = gbuf.at[mp, rows_of(o), glanes(i, who)]
        return rcopy(view, view, "gs", ((o % nz) * TURNS + i) * 2 + (0 if o else who), {"tok": sib})

    @pl.when(active)
    def _():
        for q in range(RING):
            peer_copy(q).wait_recv()

        own = jnp.concatenate([xbuf[q, rows_of(0), lanes(q)] for q in range(RING)], axis=1)
        peer = jnp.concatenate([ybuf[q, :, lanes(q)] for q in range(RING)], axis=1)
        l0 = jnp.where(mp == 0, own, peer)
        l1 = jnp.where(mp == 0, peer, own)
        lid = lax.broadcasted_iota(jnp.int32, (1, W), 1)
        counted = jnp.where((lid >= over) | (core == 0), 1.0, 0.0).astype(f32)
        lane16 = lax.broadcasted_iota(jnp.int32, (16, LANES), 1)

        def in_lanes(a, b, c):
            return jnp.where(lane16 == 0, a, jnp.where(lane16 == 1, b, c))

        h0 = jnp.max(l0, axis=1, keepdims=True)
        h1 = jnp.max(l1, axis=1, keepdims=True)
        e0 = jnp.exp(l0 - h0) * counted
        e1 = jnp.exp(l1 - h1) * counted
        stat[me, 0] = in_lanes(h0, h0, h1)
        stat[me, 1] = in_lanes(
            jnp.sum(e0, axis=1, keepdims=True), jnp.sum(e0 * (l0 - l1), axis=1, keepdims=True),
            jnp.sum(e1, axis=1, keepdims=True))

        @pl.loop(1, nv)
        def _(j):
            stat_copy(0, j).start()
            stat_copy(1, j).start()

        stat_copy(1, 0).start()

        live_total = jnp.sum(jnp.sum(mbuf[...], axis=0), axis=0, keepdims=True)[:, 1:2]
        infos = mbuf[pl.ds(2 * zi, 2)].reshape(16, LANES)
        id_col = infos[:, 0:1].astype(jnp.int32)
        coef = loss_scale * infos[:, 1:2] / live_total
        adv_col = infos[:, 2:3]
        entry = voc * vocab_dev + core * off + lid
        onehot = jnp.where(entry == id_col, 1.0, 0.0).astype(f32)

        stat_copy(1, 0).wait_recv()

        @pl.loop(1, nv)
        def _(j):
            stat_copy(0, j).wait_recv()
            stat_copy(1, j).wait_recv()

        highs = stat[:, 0]
        high = jnp.max(highs, axis=0)
        total = jnp.sum(stat[:, 1] * jnp.exp(highs - high[None]), axis=0)
        log_total = jnp.log(total)
        lse0 = high[:, 0:1] + log_total[:, 0:1]
        lse1 = high[:, 2:3] + log_total[:, 2:3]
        kl = total[:, 1:2] / total[:, 0:1] - (lse0 - lse1)

        lp0 = l0 - lse0
        diff = lp0 - (l1 - lse1)
        prob = jnp.exp(lp0)
        gbuf[mp, rows_of(0), :] = (
            coef * (adv_col * (prob - onehot) + kl_coef * prob * (diff - kl))).astype(bf16)
        for i in range(TURNS):
            for who in (0, 1):
                begin_if("active", gs_copy, 0, i, who)

    @pl.when(jnp.logical_not(active))
    def _():
        for i in range(TURNS):
            for who in (0, 1):
                gs_copy(0, i, who).wait_recv()

    def gz_copy(o, i, to):
        view = gbuf.at[mp, rows_of(o), glanes(i, core)]
        return rcopy(view, view, "gz", ((o - to) % nz) * TURNS + i, {"tok": lax.rem(tok + 2 * to + nt, nt)})

    def gz_arrival(o, i):
        view = gbuf.at[mp, rows_of(o), glanes(i, core)]
        return rcopy(view, view, "gz", (o % nz) * TURNS + i, {"tok": tok})

    def gx_copy(o, i):
        view = gbuf.at[1, rows_of(o), glanes(i, core)]
        return rcopy(view, view, "gx", (o % nz) * TURNS + i, {"mp": 1 - mp})

    def gxs_copy(o, i, who):
        view = gbuf.at[1, rows_of(o), glanes(i, who)]
        return rcopy(view, view, "gxs", (o % nz) * TURNS + i, {"tok": sib})

    def sides(d, i):
        if d == half:
            return (-1,) if i % 2 == 0 else (1,)
        return (-1, 1)

    def over_x(o, i):
        @pl.when(mp == 1)
        def _():
            begin_if("ref", gx_copy, o, i)

    for d in range(1, min(2, half) + 1):
        for i in range(TURNS):
            for side in sides(d, i):
                begin(gz_copy(0, i, -side * d))
    for i in range(TURNS):
        over_x(0, i)

    def along(d):
        for i in range(TURNS):
            for side in sides(d, i):
                o = side * d
                gz_arrival(o, i).wait_recv()
                if d == 2:
                    for more in range(3, half + 1):
                        if side in sides(more, i):
                            begin(gz_copy(o, i, -side * (more - 2)))
                begin(gs_copy(o, i, core))
                over_x(o, i)

    def across(d):
        @pl.when(mp == 0)
        def _():
            for i in range(TURNS):
                for side in sides(d, i) if d else (1,):
                    gx_copy(side * d, i).wait_recv()
                    begin_if("policy", gxs_copy, side * d, i, core)

    def sib_end(i):
        for o in range(1, nz):
            gs_copy(o, i, 1 - core).wait_recv()

    def feature(window, i):
        @pl.when(mp == 0)
        def _():
            if window == 1:
                for o in range(nz):
                    gxs_copy(o, i, 1 - core).wait_recv()
            a, n = turns[i]
            a, n = 2 * a, 2 * n
            skip = over if window == 1 and i == 0 else 0
            first = window * off
            part = lax.dot_general(
                gbuf[window, :, a + skip:a + n], wbuf[:, first + a + skip:first + a + n],
                (((1,), (1,)), ((), ())), preferred_element_type=f32).reshape(nt, 8, width)
            if window == 0 and i == 0:
                fbuf[...] = part
            else:
                fbuf[...] = fbuf[...] + part

    for d in range(1, half + 1):
        along(d)
        if d >= 2:
            across(d - 2)
    across(half - 1)
    for i in range(TURNS):
        sib_end(i)
        feature(0, i)
        if i == 0:
            across(half)
    for i in range(TURNS):
        feature(1, i)

    def fa_copy(j):
        p = lax.rem(tok + j, nt)
        return rcopy(fbuf.at[p], fabuf.at[tok], "fa", j, {"tok": p})

    def fr_copy(j):
        p = lax.rem(voc + j, nv)
        return rcopy(fabuf.at[pl.ds(p * spv, spv)], frbuf.at[voc], "fr", j, {"vocab": p})

    target = voc // (nv // 2)

    def fb_copy(j):
        p = lax.rem(voc + j, nv)
        return rcopy(fbb.at[voc], fbb.at[voc], "fb", j, {"mp": target, "vocab": p})

    def fm_copy(j, other):
        p = lax.rem(voc + j, nv)
        return rcopy(dots.at[voc], dots.at[voc], "fm", other * nv + j, {"mp": other, "vocab": p})

    def due(j):
        return lax.rem(voc - j + nv, nv) // (nv // 2) == mp

    @pl.when(mp == 0)
    def _():
        @pl.loop(1, nt)
        def _(j):
            fa_copy(j).start()

        fabuf[tok] = fbuf[tok]

    for c in (dw_copy, unit_copy, inv_copy):
        c.wait_recv()
    n_half = vocab_dev // 2
    shift = n_half - off

    def hcopy(k):
        return pltpu.make_async_copy(
            hbuf.at[pl.ds(k * kh, kh), :], head_out.at[0, pl.ds(k * kh, kh), :], hsem.at[k])

    def head_rows(k):
        dw = jnp.where(mp == 0, colb[k].astype(f32), dwb[k].astype(f32)).T.astype(bf16)
        for a, n in hpieces:
            n = min(n, n_half - a)

            @pl.when(mp == 0)
            def _():
                hbuf[k * kh:(k + 1) * kh, a:a + n] = jnp.dot(
                    dw, gbuf[0, :, a:a + n], preferred_element_type=f32).astype(bf16)

            @pl.when(mp == 1)
            def _():
                wide = min(n + LANES, W - a)
                hbuf[k * kh:(k + 1) * kh, a:a + n] = jnp.dot(
                    dw, gbuf[1, :, a:a + wide][:, shift:shift + n], preferred_element_type=f32).astype(bf16)
        hcopy(k).start()

    head_rows(0)

    @pl.when(mp == 0)
    def _():
        @pl.loop(1, nt)
        def _(j):
            fa_copy(j).wait_recv()

        @pl.loop(1, nv)
        def _(j):
            fr_copy(j).start()

        frbuf[voc] = fabuf[pl.ds(voc * spv, spv)]

    head_rows(1)

    @pl.when(mp == 0)
    def _():
        @pl.loop(1, nv)
        def _(j):
            fr_copy(j).wait_recv()

        scaled = jnp.sum(frbuf[...], axis=0) * gainb[pl.ds(voc * spv, spv)]
        mine = ubuf[pl.ds(voc * spv, spv)] * scaled
        dot = jnp.sum(jnp.sum(mine, axis=2, keepdims=True), axis=0)
        fbb[voc] = scaled
        dots[voc] = jnp.broadcast_to(dot, (8, LANES))

        @pl.loop(1, nv)
        def _(j):
            fb_copy(j).start()
            fm_copy(j, 0).start()
            fm_copy(j, 1).start()

        fm_copy(0, 1).start()

        @pl.when(target == 1)
        def _():
            fb_copy(0).start()

        @pl.loop(1, nv)
        def _(j):
            fm_copy(j, 0).wait_recv()

            @pl.when(due(j))
            def _():
                fb_copy(j).wait_recv()

    @pl.when(mp == 1)
    def _():
        @pl.loop(0, nv)
        def _(j):
            fm_copy(j, 1).wait_recv()

            @pl.when(due(j))
            def _():
                fb_copy(j).wait_recv()

    mean = jnp.sum(dots[...], axis=0)[:, 0:1] * (1.0 / (nt * width))
    inv_pol = jnp.where(mp == 0, ibuf[:, 0:1], irecv[:, 0:1])
    for i in range(nt // 2):
        slab = mp * (nt // 2) + i
        unit_pol = jnp.where(mp == 0, ubuf[i], urecv[i])
        hg_out[:, i * width:(i + 1) * width] = inv_pol * (
            fbb[slab // spv, lax.rem(slab, spv)] - unit_pol * mean)

    for k in range(2):
        hcopy(k).wait()
    for c in pending:
        c.wait_send()

    @pl.loop(1, nt)
    def _(j):
        a2a_copy(j).wait_send()
        meta_copy(j).wait_send()

    @pl.when(active)
    def _():
        stat_copy(1, 0).wait_send()

        @pl.loop(1, nv)
        def _(j):
            stat_copy(0, j).wait_send()
            stat_copy(1, j).wait_send()

    for name, cond in (
            ("active", active), ("idle", jnp.logical_not(active)), ("ref", mp == 1), ("policy", mp == 0)):
        @pl.when(cond)
        def _():
            for make, at in held[name]:
                make(*at).wait_send()

    @pl.when(mp == 0)
    def _():
        @pl.loop(1, nt)
        def _(j):
            fa_copy(j).wait_send()

        @pl.loop(1, nv)
        def _(j):
            fr_copy(j).wait_send()
            fb_copy(j).wait_send()
            fm_copy(j, 0).wait_send()
            fm_copy(j, 1).wait_send()

        fm_copy(0, 1).wait_send()

        @pl.when(target == 1)
        def _():
            fb_copy(0).wait_send()


def per_device(nt, nv, hidden, norm_gain, output_head, token_ids, live_mask, advantages):
    nz = nt // 2
    half = nz // 2
    rows, width = output_head.shape[1:]
    kh = width // 2
    blocks = rows // LANES
    W = (blocks + 1) // 2 * LANES
    piece = pieces_of(W // LANES, RING)[0][1]
    T = nt * 8
    spv = nt // nv
    plan, n_sem = sem_plan(nt, nz, nv)
    vmem = pl.BlockSpec(memory_space=pltpu.VMEM)
    smem = pl.BlockSpec(memory_space=pltpu.SMEM)
    hbm = pl.BlockSpec(memory_space=pl.ANY)
    V = pltpu.VMEM
    hg, head_part = pl.pallas_call(
        functools.partial(kernel, nt, nz, nv, plan),
        out_shape=(
            jax.ShapeDtypeStruct((8, nt // 2 * width), f32),
            jax.ShapeDtypeStruct((1, width, rows // 2), bf16),
        ),
        in_specs=[vmem, vmem, hbm, smem, smem, smem],
        out_specs=(vmem, hbm),
        scratch_shapes=[
            V((width, rows), bf16),
            V((RING, T, piece), f32),
            V((RING, T, piece), f32),
            V((RING, T, piece), f32),
            V((2, half, RING, 16, piece), f32),
            V((RING, 16, piece), f32),
            V((2, T, W), bf16),
            V((width, rows // 2), bf16),
            V((nt, 16, kh), bf16),
            V((nt, 16, kh), bf16),
            V((nt, 8, width), f32),
            V((nt // 2, 8, width), f32),
            V((8, LANES), f32),
            V((8, LANES), f32),
            V((nt, 8, width), f32),
            V((nt, 8, LANES), f32),
            V((2, T, kh), bf16),
            V((2, T, kh), bf16),
            V((2 * nv, 2, 16, LANES), f32),
            V((nt, 8, width), f32),
            V((nt, 8, width), f32),
            V((nv, spv, 8, width), f32),
            V((nv, spv, 8, width), f32),
            V((nv, 8, LANES), f32),
            pltpu.SemaphoreType.DMA((2,)),
            pltpu.SemaphoreType.DMA((2,)),
            pltpu.SemaphoreType.DMA((n_sem,)),
            pltpu.SemaphoreType.DMA((n_sem,)),
        ],
        compiler_params=pltpu.CompilerParams(
            collective_id=0, has_side_effects=True, vmem_limit_bytes=56 * 2**20),
        cost_estimate=pl.CostEstimate(
            flops=5 * rows * width * T, bytes_accessed=3 * rows * width, transcendentals=3 * 16 * W),
    )(hidden, norm_gain, jnp.swapaxes(output_head, 1, 2), token_ids, live_mask, advantages)
    return hg, jnp.swapaxes(head_part, 1, 2)


def solution(mesh):
    placed = (
        P("mp", "tok", None),
        P("mp", None),
        P("mp", "vocab", "tok"),
        P("tok"),
        P("tok"),
        P("tok"),
    )
    return jax.shard_map(
        functools.partial(per_device, mesh.shape["tok"], mesh.shape["vocab"]),
        mesh=mesh,
        in_specs=placed,
        out_specs=(P("tok", "mp"), P("mp", "vocab", "tok")),
        check_vma=False,
    )
```

```python
import functools

import jax
import jax.numpy as jnp
from jax import lax
from jax.experimental import pallas as pl
from jax.experimental.pallas import tpu as pltpu
from jax.sharding import PartitionSpec as P

loss_scale = 256.0
kl_coef = 0.1
norm_eps = 1e-06
MESH = pl.DeviceIdType.MESH
f32 = jnp.float32
bf16 = jnp.bfloat16
LANES = 128


def pieces_of(blocks, number):
    sizes = [(blocks + number - 1 - i) // number for i in range(number)]
    starts = [sum(sizes[:i]) for i in range(number)]
    return [(a * LANES, n * LANES) for a, n in zip(starts, sizes)]


RING = 8
TURNS = 2
LEAD = 5
READY = 2
HEAD_PARTS = 4


def sem_plan(nt, nz, nv):
    sizes = dict(
        a2a=nt, meta=nt, dw=1, unit=1, inv=1, pair=RING, up=RING * nz, down=RING * nz, peer=RING, stat=2 * nv, gs=2 * TURNS * nz,
        gz=TURNS * nz, gx=TURNS * nz, gxs=TURNS * nz, fa=nt, fr=nv, fb=nv, fm=2 * nv)
    plan, count = {}, 0
    for name, size in sizes.items():
        plan[name] = count
        count += size
    return plan, count


def kernel(nt, nz, nv, plan,
           hidden, gain, head, ids, live, adv,
           hg_out, head_out,
           wbuf, lsib, lown, xbuf, rbuf, ybuf, gbuf, hbuf,
           nbuf, cbuf, ubuf, urecv, ibuf, irecv, gainb, mbuf, colb, dwb,
           stat, fbuf, fabuf, frbuf, fbb, dots,
           wsem, hsem, ss, rs):
    mp = lax.axis_index("mp")
    tok = lax.axis_index("tok")
    voc = lax.axis_index("vocab")
    zi = tok // 2
    core = tok % 2
    sib = tok + 1 - 2 * core
    half = nz // 2
    T = nt * 8
    width, vocab_dev = wbuf.shape
    kh = width // 2
    W = gbuf.shape[2]
    off = vocab_dev - W
    over = W - off
    spv = nt // nv
    rpieces = pieces_of(W // LANES, RING)
    turns = pieces_of(W // LANES // 2, TURNS)
    hpieces = pieces_of(W // LANES, HEAD_PARTS)
    active = mp == core
    held = {}
    pending = []

    def rcopy(src, dst, name, index, dev):
        at = plan[name] + index
        return pltpu.make_async_remote_copy(
            src_ref=src, dst_ref=dst, send_sem=ss.at[at], recv_sem=rs.at[at],
            device_id=dev, device_id_type=MESH)

    def begin(c):
        c.start()
        pending.append(c)

    def begin_if(when, make, *at):
        make(*at).start()
        held.setdefault(when, []).append((make, at))

    def zat(o):
        return lax.rem(zi + o + nz, nz)

    def rows_of(o):
        return pl.ds(pl.multiple_of(zat(o) * 16, 16), 16)

    def way_dev(way):
        return {"tok": lax.rem(tok + (2 if way == "up" else nt - 2), nt)}

    def wcopy(k):
        return pltpu.make_async_copy(
            head.at[0, pl.ds(k * kh, kh), :], wbuf.at[pl.ds(k * kh, kh), :], wsem.at[k])

    for k in range(2):
        wcopy(k).start()

    barrier = pltpu.get_barrier_semaphore()

    def greet(dev):
        pl.semaphore_signal(barrier, inc=1, device_id=dev, device_id_type=MESH)

    @pl.loop(1, nt)
    def _(j):
        greet({"tok": lax.rem(tok + j, nt)})

    @pl.loop(1, nv)
    def _(j):
        greet({"vocab": lax.rem(voc + j, nv)})

    @pl.loop(0, nv)
    def _(j):
        greet({"mp": 1 - mp, "vocab": lax.rem(voc + j, nv)})
        greet({"mp": 1 - mp, "tok": sib, "vocab": lax.rem(voc + j, nv)})

    x = hidden[0].astype(f32)
    inv = lax.rsqrt(jnp.mean(x * x, axis=1, keepdims=True) + norm_eps)
    unit = x * inv
    g = gain[...]
    normed = unit * g
    for k in range(nt):
        a = k * width
        nbuf[k] = jnp.concatenate(
            [normed[:, a:a + kh], normed[:, a + kh:a + width]], axis=0).astype(bf16)
    cbuf[tok] = nbuf[tok]

    pl.semaphore_wait(barrier, nt - 1 + nv - 1 + 2 * nv)

    def a2a_copy(j):
        p = lax.rem(tok + j, nt)
        return rcopy(nbuf.at[p], cbuf.at[tok], "a2a", j, {"tok": p})

    def meta_copy(j):
        p = lax.rem(tok + j, nt)
        return rcopy(mbuf.at[tok], mbuf.at[tok], "meta", j, {"tok": p})

    @pl.loop(1, nt)
    def _(j):
        a2a_copy(j).start()

    for k in range(nt):
        cols = slice(k * width, (k + 1) * width)
        ubuf[k] = unit[:, cols]
        gainb[k] = jnp.broadcast_to(g[:, cols], (8, width))
    ibuf[...] = jnp.broadcast_to(inv, ibuf.shape)
    lane = lax.broadcasted_iota(jnp.int32, (8, LANES), 1)
    row = lax.broadcasted_iota(jnp.int32, (8, LANES), 0)
    info = jnp.zeros((8, LANES), f32)
    for j in range(8):
        mine = jnp.where(lane == 0, ids[j].astype(f32), jnp.where(lane == 1, live[j].astype(f32), adv[j]))
        info = jnp.where(row == j, mine, info)
    mbuf[tok] = info

    @pl.loop(1, nt)
    def _(j):
        meta_copy(j).start()

    for k in range(2):
        wcopy(k).wait()

    @pl.loop(1, nt)
    def _(j):
        a2a_copy(j).wait_recv()

    cols = cbuf[...].astype(f32)
    colb[0] = cols[:, 0:8, :].reshape(T, kh).astype(bf16)
    colb[1] = cols[:, 8:16, :].reshape(T, kh).astype(bf16)

    def dot_piece(window, q):
        a, n = rpieces[q]
        at = pl.ds(pl.multiple_of(window * off + a, LANES), n)
        return jnp.dot(colb[0], wbuf[0:kh, at], preferred_element_type=f32) + jnp.dot(
            colb[1], wbuf[kh:width, at], preferred_element_type=f32)

    def lanes(q):
        return pl.ds(0, rpieces[q][1])

    def glanes(i, who):
        a, n = turns[i]
        return pl.ds(pl.multiple_of(2 * a + who * n, LANES), n)

    def pair_copy(q):
        return rcopy(lsib.at[q, :, lanes(q)], xbuf.at[q, :, lanes(q)], "pair", q, {"tok": sib})

    def logits(q):
        lsib[q, :, lanes(q)] = dot_piece(1 - core, q)
        begin(pair_copy(q))
        lown[q, :, lanes(q)] = dot_piece(core, q)

    def chain(way, q):
        first = half if (way == "up") == (q % 2 == 0) else half - 1
        return list(range(first, 0, -1))

    def ring_copy(way, d, q):
        o = d if way == "up" else -d
        w = 0 if way == "up" else 1
        return rcopy(
            xbuf.at[q, rows_of(o), lanes(q)], rbuf.at[w, d - 1, q, :, lanes(q)], way, (d - 1) * RING + q, way_dev(way))

    done = {}

    def peer_copy(q):
        return rcopy(xbuf.at[q, rows_of(0), lanes(q)], ybuf.at[q, :, lanes(q)], "peer", q, {"mp": 1 - mp})

    def logits_ready(q):
        pair_copy(q).wait_recv()
        xbuf[q, :, lanes(q)] = xbuf[q, :, lanes(q)] + lown[q, :, lanes(q)]
        for way in ("up", "down"):
            begin(ring_copy(way, chain(way, q)[0], q))
        done[q] = 0

    def step(way, q, hop):
        ds = chain(way, q)
        if hop > len(ds):
            return
        d = ds[hop - 1]
        ring_copy(way, d, q).wait_recv()
        o = d - 1 if way == "up" else 1 - d
        w = 0 if way == "up" else 1
        xbuf[q, rows_of(o), lanes(q)] = xbuf[q, rows_of(o), lanes(q)] + rbuf[w, d - 1, q, :, lanes(q)]
        if d > 1:
            begin(ring_copy(way, d - 1, q))
            return
        done[q] += 1
        if done[q] == 2:
            @pl.when(jnp.logical_not(active))
            def _():
                begin_if("idle", peer_copy, q)

    dw_copy = rcopy(colb, dwb, "dw", 0, {"mp": 1 - mp})
    unit_copy = rcopy(ubuf.at[pl.ds(nt // 2, nt // 2)], urecv, "unit", 0, {"mp": 1 - mp})
    inv_copy = rcopy(ibuf, irecv, "inv", 0, {"mp": 1 - mp})

    def steps(hop, q):
        step("up", q, hop)
        step("down", q, hop)

    lead = LEAD
    for q in range(RING):
        logits(q)
        if q >= READY:
            logits_ready(q - READY)
        if q == 3:
            for c in (dw_copy, unit_copy, inv_copy):
                begin(c)
        if q >= lead:
            steps(1, q - lead)
    for q in range(RING - READY, RING):
        logits_ready(q)

    for hop in range(1, half + 1):
        for q in range(RING):
            if hop > 1 or q >= RING - lead:
                steps(hop, q)

    @pl.loop(1, nt)
    def _(j):
        meta_copy(j).wait_recv()

    me = mp * nv + voc

    def stat_copy(other, j):
        dev = {"vocab": lax.rem(voc + j, nv)}
        if other:
            dev.update({"mp": 1 - mp, "tok": sib})
        return rcopy(stat.at[me], stat.at[me], "stat", other * nv + j, dev)

    def gs_copy(o, i, who):
        view = gbuf.at[mp, rows_of(o), glanes(i, who)]
        return rcopy(view, view, "gs", ((o % nz) * TURNS + i) * 2 + (0 if o else who), {"tok": sib})

    @pl.when(active)
    def _():
        for q in range(RING):
            peer_copy(q).wait_recv()

        own = jnp.concatenate([xbuf[q, rows_of(0), lanes(q)] for q in range(RING)], axis=1)
        peer = jnp.concatenate([ybuf[q, :, lanes(q)] for q in range(RING)], axis=1)
        l0 = jnp.where(mp == 0, own, peer)
        l1 = jnp.where(mp == 0, peer, own)
        lid = lax.broadcasted_iota(jnp.int32, (1, W), 1)
        counted = jnp.where((lid >= over) | (core == 0), 1.0, 0.0).astype(f32)
        lane16 = lax.broadcasted_iota(jnp.int32, (16, LANES), 1)

        def in_lanes(a, b, c):
            return jnp.where(lane16 == 0, a, jnp.where(lane16 == 1, b, c))

        h0 = jnp.max(l0, axis=1, keepdims=True)
        h1 = jnp.max(l1, axis=1, keepdims=True)
        e0 = jnp.exp(l0 - h0) * counted
        e1 = jnp.exp(l1 - h1) * counted
        stat[me, 0] = in_lanes(h0, h0, h1)
        stat[me, 1] = in_lanes(
            jnp.sum(e0, axis=1, keepdims=True), jnp.sum(e0 * (l0 - l1), axis=1, keepdims=True),
            jnp.sum(e1, axis=1, keepdims=True))

        @pl.loop(1, nv)
        def _(j):
            stat_copy(0, j).start()
            stat_copy(1, j).start()

        stat_copy(1, 0).start()

        live_total = jnp.sum(jnp.sum(mbuf[...], axis=0), axis=0, keepdims=True)[:, 1:2]
        infos = mbuf[pl.ds(2 * zi, 2)].reshape(16, LANES)
        id_col = infos[:, 0:1].astype(jnp.int32)
        coef = loss_scale * infos[:, 1:2] / live_total
        adv_col = infos[:, 2:3]
        entry = voc * vocab_dev + core * off + lid
        onehot = jnp.where(entry == id_col, 1.0, 0.0).astype(f32)

        stat_copy(1, 0).wait_recv()

        @pl.loop(1, nv)
        def _(j):
            stat_copy(0, j).wait_recv()
            stat_copy(1, j).wait_recv()

        highs = stat[:, 0]
        high = jnp.max(highs, axis=0)
        total = jnp.sum(stat[:, 1] * jnp.exp(highs - high[None]), axis=0)
        log_total = jnp.log(total)
        lse0 = high[:, 0:1] + log_total[:, 0:1]
        lse1 = high[:, 2:3] + log_total[:, 2:3]
        kl = total[:, 1:2] / total[:, 0:1] - (lse0 - lse1)

        lp0 = l0 - lse0
        diff = lp0 - (l1 - lse1)
        prob = jnp.exp(lp0)
        gbuf[mp, rows_of(0), :] = (
            coef * (adv_col * (prob - onehot) + kl_coef * prob * (diff - kl))).astype(bf16)
        for i in range(TURNS):
            for who in (0, 1):
                begin_if("active", gs_copy, 0, i, who)

    @pl.when(jnp.logical_not(active))
    def _():
        for i in range(TURNS):
            for who in (0, 1):
                gs_copy(0, i, who).wait_recv()

    def gz_copy(o, i, to):
        view = gbuf.at[mp, rows_of(o), glanes(i, core)]
        return rcopy(view, view, "gz", ((o - to) % nz) * TURNS + i, {"tok": lax.rem(tok + 2 * to + nt, nt)})

    def gz_arrival(o, i):
        view = gbuf.at[mp, rows_of(o), glanes(i, core)]
        return rcopy(view, view, "gz", (o % nz) * TURNS + i, {"tok": tok})

    def gx_copy(o, i):
        view = gbuf.at[1, rows_of(o), glanes(i, core)]
        return rcopy(view, view, "gx", (o % nz) * TURNS + i, {"mp": 1 - mp})

    def gxs_copy(o, i, who):
        view = gbuf.at[1, rows_of(o), glanes(i, who)]
        return rcopy(view, view, "gxs", (o % nz) * TURNS + i, {"tok": sib})

    def sides(d, i):
        if d == half:
            return (-1,) if i % 2 == 0 else (1,)
        return (-1, 1)

    def over_x(o, i):
        @pl.when(mp == 1)
        def _():
            begin_if("ref", gx_copy, o, i)

    for d in range(1, min(2, half) + 1):
        for i in range(TURNS):
            for side in sides(d, i):
                begin(gz_copy(0, i, -side * d))
    for i in range(TURNS):
        over_x(0, i)

    def along(d):
        for i in range(TURNS):
            for side in sides(d, i):
                o = side * d
                gz_arrival(o, i).wait_recv()
                if d == 2:
                    for more in range(3, half + 1):
                        if side in sides(more, i):
                            begin(gz_copy(o, i, -side * (more - 2)))
                begin(gs_copy(o, i, core))
                over_x(o, i)

    def across(d):
        @pl.when(mp == 0)
        def _():
            for i in range(TURNS):
                for side in sides(d, i) if d else (1,):
                    gx_copy(side * d, i).wait_recv()
                    begin_if("policy", gxs_copy, side * d, i, core)

    def sib_end(i):
        for o in range(1, nz):
            gs_copy(o, i, 1 - core).wait_recv()

    def feature(window, i):
        @pl.when(mp == 0)
        def _():
            if window == 1:
                for o in range(nz):
                    gxs_copy(o, i, 1 - core).wait_recv()
            a, n = turns[i]
            a, n = 2 * a, 2 * n
            skip = over if window == 1 and i == 0 else 0
            first = window * off
            part = lax.dot_general(
                gbuf[window, :, a + skip:a + n], wbuf[:, first + a + skip:first + a + n],
                (((1,), (1,)), ((), ())), preferred_element_type=f32).reshape(nt, 8, width)
            if window == 0 and i == 0:
                fbuf[...] = part
            else:
                fbuf[...] = fbuf[...] + part

    for d in range(1, half + 1):
        along(d)
        if d >= 2:
            across(d - 2)
    across(half - 1)
    for i in range(TURNS):
        sib_end(i)
        feature(0, i)
        if i == 0:
            across(half)
    for i in range(TURNS):
        feature(1, i)

    def fa_copy(j):
        p = lax.rem(tok + j, nt)
        return rcopy(fbuf.at[p], fabuf.at[tok], "fa", j, {"tok": p})

    def fr_copy(j):
        p = lax.rem(voc + j, nv)
        return rcopy(fabuf.at[pl.ds(p * spv, spv)], frbuf.at[voc], "fr", j, {"vocab": p})

    target = voc // (nv // 2)

    def fb_copy(j):
        p = lax.rem(voc + j, nv)
        return rcopy(fbb.at[voc], fbb.at[voc], "fb", j, {"mp": target, "vocab": p})

    def fm_copy(j, other):
        p = lax.rem(voc + j, nv)
        return rcopy(dots.at[voc], dots.at[voc], "fm", other * nv + j, {"mp": other, "vocab": p})

    def due(j):
        return lax.rem(voc - j + nv, nv) // (nv // 2) == mp

    @pl.when(mp == 0)
    def _():
        @pl.loop(1, nt)
        def _(j):
            fa_copy(j).start()

        fabuf[tok] = fbuf[tok]

    for c in (dw_copy, unit_copy, inv_copy):
        c.wait_recv()
    n_half = vocab_dev // 2
    shift = n_half - off

    def hcopy(k):
        return pltpu.make_async_copy(
            hbuf.at[pl.ds(k * kh, kh), :], head_out.at[0, pl.ds(k * kh, kh), :], hsem.at[k])

    def head_rows(k):
        dw = jnp.where(mp == 0, colb[k].astype(f32), dwb[k].astype(f32)).T.astype(bf16)
        for a, n in hpieces:
            n = min(n, n_half - a)

            @pl.when(mp == 0)
            def _():
                hbuf[k * kh:(k + 1) * kh, a:a + n] = jnp.dot(
                    dw, gbuf[0, :, a:a + n], preferred_element_type=f32).astype(bf16)

            @pl.when(mp == 1)
            def _():
                wide = min(n + LANES, W - a)
                hbuf[k * kh:(k + 1) * kh, a:a + n] = jnp.dot(
                    dw, gbuf[1, :, a:a + wide][:, shift:shift + n], preferred_element_type=f32).astype(bf16)
        hcopy(k).start()

    head_rows(0)

    @pl.when(mp == 0)
    def _():
        @pl.loop(1, nt)
        def _(j):
            fa_copy(j).wait_recv()

        @pl.loop(1, nv)
        def _(j):
            fr_copy(j).start()

        frbuf[voc] = fabuf[pl.ds(voc * spv, spv)]

    head_rows(1)

    @pl.when(mp == 0)
    def _():
        @pl.loop(1, nv)
        def _(j):
            fr_copy(j).wait_recv()

        scaled = jnp.sum(frbuf[...], axis=0) * gainb[pl.ds(voc * spv, spv)]
        mine = ubuf[pl.ds(voc * spv, spv)] * scaled
        dot = jnp.sum(jnp.sum(mine, axis=2, keepdims=True), axis=0)
        fbb[voc] = scaled
        dots[voc] = jnp.broadcast_to(dot, (8, LANES))

        @pl.loop(1, nv)
        def _(j):
            fb_copy(j).start()
            fm_copy(j, 0).start()
            fm_copy(j, 1).start()

        fm_copy(0, 1).start()

        @pl.when(target == 1)
        def _():
            fb_copy(0).start()

        @pl.loop(1, nv)
        def _(j):
            fm_copy(j, 0).wait_recv()

            @pl.when(due(j))
            def _():
                fb_copy(j).wait_recv()

    @pl.when(mp == 1)
    def _():
        @pl.loop(0, nv)
        def _(j):
            fm_copy(j, 1).wait_recv()

            @pl.when(due(j))
            def _():
                fb_copy(j).wait_recv()

    mean = jnp.sum(dots[...], axis=0)[:, 0:1] * (1.0 / (nt * width))
    inv_pol = jnp.where(mp == 0, ibuf[:, 0:1], irecv[:, 0:1])
    for i in range(nt // 2):
        slab = mp * (nt // 2) + i
        unit_pol = jnp.where(mp == 0, ubuf[i], urecv[i])
        hg_out[:, i * width:(i + 1) * width] = inv_pol * (
            fbb[slab // spv, lax.rem(slab, spv)] - unit_pol * mean)

    for k in range(2):
        hcopy(k).wait()
    for c in pending:
        c.wait_send()

    @pl.loop(1, nt)
    def _(j):
        a2a_copy(j).wait_send()
        meta_copy(j).wait_send()

    @pl.when(active)
    def _():
        stat_copy(1, 0).wait_send()

        @pl.loop(1, nv)
        def _(j):
            stat_copy(0, j).wait_send()
            stat_copy(1, j).wait_send()

    for name, cond in (
            ("active", active), ("idle", jnp.logical_not(active)), ("ref", mp == 1), ("policy", mp == 0)):
        @pl.when(cond)
        def _():
            for make, at in held[name]:
                make(*at).wait_send()

    @pl.when(mp == 0)
    def _():
        @pl.loop(1, nt)
        def _(j):
            fa_copy(j).wait_send()

        @pl.loop(1, nv)
        def _(j):
            fr_copy(j).wait_send()
            fb_copy(j).wait_send()
            fm_copy(j, 0).wait_send()
            fm_copy(j, 1).wait_send()

        fm_copy(0, 1).wait_send()

        @pl.when(target == 1)
        def _():
            fb_copy(0).wait_send()


def per_device(nt, nv, hidden, norm_gain, output_head, token_ids, live_mask, advantages):
    nz = nt // 2
    half = nz // 2
    rows, width = output_head.shape[1:]
    kh = width // 2
    blocks = rows // LANES
    W = (blocks + 1) // 2 * LANES
    piece = pieces_of(W // LANES, RING)[0][1]
    T = nt * 8
    spv = nt // nv
    plan, n_sem = sem_plan(nt, nz, nv)
    vmem = pl.BlockSpec(memory_space=pltpu.VMEM)
    smem = pl.BlockSpec(memory_space=pltpu.SMEM)
    hbm = pl.BlockSpec(memory_space=pl.ANY)
    V = pltpu.VMEM
    hg, head_part = pl.pallas_call(
        functools.partial(kernel, nt, nz, nv, plan),
        out_shape=(
            jax.ShapeDtypeStruct((8, nt // 2 * width), f32),
            jax.ShapeDtypeStruct((1, width, rows // 2), bf16),
        ),
        in_specs=[vmem, vmem, hbm, smem, smem, smem],
        out_specs=(vmem, hbm),
        scratch_shapes=[
            V((width, rows), bf16),
            V((RING, T, piece), f32),
            V((RING, T, piece), f32),
            V((RING, T, piece), f32),
            V((2, half, RING, 16, piece), f32),
            V((RING, 16, piece), f32),
            V((2, T, W), bf16),
            V((width, rows // 2), bf16),
            V((nt, 16, kh), bf16),
            V((nt, 16, kh), bf16),
            V((nt, 8, width), f32),
            V((nt // 2, 8, width), f32),
            V((8, LANES), f32),
            V((8, LANES), f32),
            V((nt, 8, width), f32),
            V((nt, 8, LANES), f32),
            V((2, T, kh), bf16),
            V((2, T, kh), bf16),
            V((2 * nv, 2, 16, LANES), f32),
            V((nt, 8, width), f32),
            V((nt, 8, width), f32),
            V((nv, spv, 8, width), f32),
            V((nv, spv, 8, width), f32),
            V((nv, 8, LANES), f32),
            pltpu.SemaphoreType.DMA((2,)),
            pltpu.SemaphoreType.DMA((2,)),
            pltpu.SemaphoreType.DMA((n_sem,)),
            pltpu.SemaphoreType.DMA((n_sem,)),
        ],
        compiler_params=pltpu.CompilerParams(
            collective_id=0, has_side_effects=True, vmem_limit_bytes=56 * 2**20),
        cost_estimate=pl.CostEstimate(
            flops=5 * rows * width * T, bytes_accessed=3 * rows * width, transcendentals=3 * 16 * W),
    )(hidden, norm_gain, jnp.swapaxes(output_head, 1, 2), token_ids, live_mask, advantages)
    return hg, jnp.swapaxes(head_part, 1, 2)


def solution(mesh):
    placed = (
        P("mp", "tok", None),
        P("mp", None),
        P("mp", "vocab", "tok"),
        P("tok"),
        P("tok"),
        P("tok"),
    )
    return jax.shard_map(
        functools.partial(per_device, mesh.shape["tok"], mesh.shape["vocab"]),
        mesh=mesh,
        in_specs=placed,
        out_specs=(P("tok", "mp"), P("mp", "vocab", "tok")),
        check_vma=False,
    )
```

```python
import functools

import jax
import jax.numpy as jnp
from jax import lax
from jax.experimental import pallas as pl
from jax.experimental.pallas import tpu as pltpu
from jax.sharding import PartitionSpec as P

loss_scale = 256.0
kl_coef = 0.1
norm_eps = 1e-06
MESH = pl.DeviceIdType.MESH
f32 = jnp.float32
bf16 = jnp.bfloat16
LANES = 128


def pieces_of(blocks, number):
    sizes = [(blocks + number - 1 - i) // number for i in range(number)]
    starts = [sum(sizes[:i]) for i in range(number)]
    return [(a * LANES, n * LANES) for a, n in zip(starts, sizes)]


RING = 8
TURNS = 1
LEAD = 5
READY = 2
HEAD_PARTS = 4


def sem_plan(nt, nz, nv):
    sizes = dict(
        a2a=nt, meta=nt, dw=1, unit=1, inv=1, pair=RING, up=RING * nz, down=RING * nz, peer=RING, stat=2 * nv, gs=2 * TURNS * nz,
        gz=TURNS * nz, gx=TURNS * nz, gxs=TURNS * nz, fa=nt, fr=nv, fb=nv, fm=2 * nv)
    plan, count = {}, 0
    for name, size in sizes.items():
        plan[name] = count
        count += size
    return plan, count


def kernel(nt, nz, nv, plan,
           hidden, gain, head, ids, live, adv,
           hg_out, head_out,
           wbuf, lsib, lown, xbuf, rbuf, ybuf, gbuf, hbuf,
           nbuf, cbuf, ubuf, urecv, ibuf, irecv, gainb, mbuf, colb, dwb,
           stat, fbuf, fabuf, frbuf, fbb, dots,
           wsem, hsem, ss, rs):
    mp = lax.axis_index("mp")
    tok = lax.axis_index("tok")
    voc = lax.axis_index("vocab")
    zi = tok // 2
    core = tok % 2
    sib = tok + 1 - 2 * core
    half = nz // 2
    T = nt * 8
    width, vocab_dev = wbuf.shape
    kh = width // 2
    W = gbuf.shape[2]
    off = vocab_dev - W
    over = W - off
    spv = nt // nv
    rpieces = pieces_of(W // LANES, RING)
    turns = pieces_of(W // LANES // 2, TURNS)
    hpieces = pieces_of(W // LANES, HEAD_PARTS)
    active = mp == core
    held = {}
    pending = []

    def rcopy(src, dst, name, index, dev):
        at = plan[name] + index
        return pltpu.make_async_remote_copy(
            src_ref=src, dst_ref=dst, send_sem=ss.at[at], recv_sem=rs.at[at],
            device_id=dev, device_id_type=MESH)

    def begin(c):
        c.start()
        pending.append(c)

    def begin_if(when, make, *at):
        make(*at).start()
        held.setdefault(when, []).append((make, at))

    def zat(o):
        return lax.rem(zi + o + nz, nz)

    def rows_of(o):
        return pl.ds(pl.multiple_of(zat(o) * 16, 16), 16)

    def way_dev(way):
        return {"tok": lax.rem(tok + (2 if way == "up" else nt - 2), nt)}

    def wcopy(k):
        return pltpu.make_async_copy(
            head.at[0, pl.ds(k * kh, kh), :], wbuf.at[pl.ds(k * kh, kh), :], wsem.at[k])

    for k in range(2):
        wcopy(k).start()

    barrier = pltpu.get_barrier_semaphore()

    def greet(dev):
        pl.semaphore_signal(barrier, inc=1, device_id=dev, device_id_type=MESH)

    @pl.loop(1, nt)
    def _(j):
        greet({"tok": lax.rem(tok + j, nt)})

    @pl.loop(1, nv)
    def _(j):
        greet({"vocab": lax.rem(voc + j, nv)})

    @pl.loop(0, nv)
    def _(j):
        greet({"mp": 1 - mp, "vocab": lax.rem(voc + j, nv)})
        greet({"mp": 1 - mp, "tok": sib, "vocab": lax.rem(voc + j, nv)})

    x = hidden[0].astype(f32)
    inv = lax.rsqrt(jnp.mean(x * x, axis=1, keepdims=True) + norm_eps)
    unit = x * inv
    g = gain[...]
    normed = unit * g
    for k in range(nt):
        a = k * width
        nbuf[k] = jnp.concatenate(
            [normed[:, a:a + kh], normed[:, a + kh:a + width]], axis=0).astype(bf16)
    cbuf[tok] = nbuf[tok]

    pl.semaphore_wait(barrier, nt - 1 + nv - 1 + 2 * nv)

    def a2a_copy(j):
        p = lax.rem(tok + j, nt)
        return rcopy(nbuf.at[p], cbuf.at[tok], "a2a", j, {"tok": p})

    def meta_copy(j):
        p = lax.rem(tok + j, nt)
        return rcopy(mbuf.at[tok], mbuf.at[tok], "meta", j, {"tok": p})

    @pl.loop(1, nt)
    def _(j):
        a2a_copy(j).start()

    for k in range(nt):
        cols = slice(k * width, (k + 1) * width)
        ubuf[k] = unit[:, cols]
        gainb[k] = jnp.broadcast_to(g[:, cols], (8, width))
    ibuf[...] = jnp.broadcast_to(inv, ibuf.shape)
    lane = lax.broadcasted_iota(jnp.int32, (8, LANES), 1)
    row = lax.broadcasted_iota(jnp.int32, (8, LANES), 0)
    info = jnp.zeros((8, LANES), f32)
    for j in range(8):
        mine = jnp.where(lane == 0, ids[j].astype(f32), jnp.where(lane == 1, live[j].astype(f32), adv[j]))
        info = jnp.where(row == j, mine, info)
    mbuf[tok] = info

    @pl.loop(1, nt)
    def _(j):
        meta_copy(j).start()

    for k in range(2):
        wcopy(k).wait()

    @pl.loop(1, nt)
    def _(j):
        a2a_copy(j).wait_recv()

    cols = cbuf[...].astype(f32)
    colb[0] = cols[:, 0:8, :].reshape(T, kh).astype(bf16)
    colb[1] = cols[:, 8:16, :].reshape(T, kh).astype(bf16)

    def dot_piece(window, q):
        a, n = rpieces[q]
        at = pl.ds(pl.multiple_of(window * off + a, LANES), n)
        return jnp.dot(colb[0], wbuf[0:kh, at], preferred_element_type=f32) + jnp.dot(
            colb[1], wbuf[kh:width, at], preferred_element_type=f32)

    def lanes(q):
        return pl.ds(0, rpieces[q][1])

    def glanes(i, who):
        a, n = turns[i]
        return pl.ds(pl.multiple_of(2 * a + who * n, LANES), n)

    def pair_copy(q):
        return rcopy(lsib.at[q, :, lanes(q)], xbuf.at[q, :, lanes(q)], "pair", q, {"tok": sib})

    def logits(q):
        lsib[q, :, lanes(q)] = dot_piece(1 - core, q)
        begin(pair_copy(q))
        lown[q, :, lanes(q)] = dot_piece(core, q)

    def chain(way, q):
        first = half if (way == "up") == (q % 2 == 0) else half - 1
        return list(range(first, 0, -1))

    def ring_copy(way, d, q):
        o = d if way == "up" else -d
        w = 0 if way == "up" else 1
        return rcopy(
            xbuf.at[q, rows_of(o), lanes(q)], rbuf.at[w, d - 1, q, :, lanes(q)], way, (d - 1) * RING + q, way_dev(way))

    done = {}

    def peer_copy(q):
        return rcopy(xbuf.at[q, rows_of(0), lanes(q)], ybuf.at[q, :, lanes(q)], "peer", q, {"mp": 1 - mp})

    def logits_ready(q):
        pair_copy(q).wait_recv()
        xbuf[q, :, lanes(q)] = xbuf[q, :, lanes(q)] + lown[q, :, lanes(q)]
        for way in ("up", "down"):
            begin(ring_copy(way, chain(way, q)[0], q))
        done[q] = 0

    def step(way, q, hop):
        ds = chain(way, q)
        if hop > len(ds):
            return
        d = ds[hop - 1]
        ring_copy(way, d, q).wait_recv()
        o = d - 1 if way == "up" else 1 - d
        w = 0 if way == "up" else 1
        xbuf[q, rows_of(o), lanes(q)] = xbuf[q, rows_of(o), lanes(q)] + rbuf[w, d - 1, q, :, lanes(q)]
        if d > 1:
            begin(ring_copy(way, d - 1, q))
            return
        done[q] += 1
        if done[q] == 2:
            @pl.when(jnp.logical_not(active))
            def _():
                begin_if("idle", peer_copy, q)

    dw_copy = rcopy(colb, dwb, "dw", 0, {"mp": 1 - mp})
    unit_copy = rcopy(ubuf.at[pl.ds(nt // 2, nt // 2)], urecv, "unit", 0, {"mp": 1 - mp})
    inv_copy = rcopy(ibuf, irecv, "inv", 0, {"mp": 1 - mp})

    def steps(hop, q):
        step("up", q, hop)
        step("down", q, hop)

    lead = LEAD
    for q in range(RING):
        logits(q)
        if q >= READY:
            logits_ready(q - READY)
        if q == 3:
            for c in (dw_copy, unit_copy, inv_copy):
                begin(c)
        if q >= lead:
            steps(1, q - lead)
    for q in range(RING - READY, RING):
        logits_ready(q)

    for hop in range(1, half + 1):
        for q in range(RING):
            if hop > 1 or q >= RING - lead:
                steps(hop, q)

    @pl.loop(1, nt)
    def _(j):
        meta_copy(j).wait_recv()

    me = mp * nv + voc

    def stat_copy(other, j):
        dev = {"vocab": lax.rem(voc + j, nv)}
        if other:
            dev.update({"mp": 1 - mp, "tok": sib})
        return rcopy(stat.at[me], stat.at[me], "stat", other * nv + j, dev)

    def gs_copy(o, i, who):
        view = gbuf.at[mp, rows_of(o), glanes(i, who)]
        return rcopy(view, view, "gs", ((o % nz) * TURNS + i) * 2 + (0 if o else who), {"tok": sib})

    @pl.when(active)
    def _():
        for q in range(RING):
            peer_copy(q).wait_recv()

        own = jnp.concatenate([xbuf[q, rows_of(0), lanes(q)] for q in range(RING)], axis=1)
        peer = jnp.concatenate([ybuf[q, :, lanes(q)] for q in range(RING)], axis=1)
        l0 = jnp.where(mp == 0, own, peer)
        l1 = jnp.where(mp == 0, peer, own)
        lid = lax.broadcasted_iota(jnp.int32, (1, W), 1)
        counted = jnp.where((lid >= over) | (core == 0), 1.0, 0.0).astype(f32)
        lane16 = lax.broadcasted_iota(jnp.int32, (16, LANES), 1)

        def in_lanes(a, b, c):
            return jnp.where(lane16 == 0, a, jnp.where(lane16 == 1, b, c))

        h0 = jnp.max(l0, axis=1, keepdims=True)
        h1 = jnp.max(l1, axis=1, keepdims=True)
        e0 = jnp.exp(l0 - h0) * counted
        e1 = jnp.exp(l1 - h1) * counted
        stat[me, 0] = in_lanes(h0, h0, h1)
        stat[me, 1] = in_lanes(
            jnp.sum(e0, axis=1, keepdims=True), jnp.sum(e0 * (l0 - l1), axis=1, keepdims=True),
            jnp.sum(e1, axis=1, keepdims=True))

        @pl.loop(1, nv)
        def _(j):
            stat_copy(0, j).start()
            stat_copy(1, j).start()

        stat_copy(1, 0).start()

        live_total = jnp.sum(jnp.sum(mbuf[...], axis=0), axis=0, keepdims=True)[:, 1:2]
        infos = mbuf[pl.ds(2 * zi, 2)].reshape(16, LANES)
        id_col = infos[:, 0:1].astype(jnp.int32)
        coef = loss_scale * infos[:, 1:2] / live_total
        adv_col = infos[:, 2:3]
        entry = voc * vocab_dev + core * off + lid
        onehot = jnp.where(entry == id_col, 1.0, 0.0).astype(f32)

        stat_copy(1, 0).wait_recv()

        @pl.loop(1, nv)
        def _(j):
            stat_copy(0, j).wait_recv()
            stat_copy(1, j).wait_recv()

        highs = stat[:, 0]
        high = jnp.max(highs, axis=0)
        total = jnp.sum(stat[:, 1] * jnp.exp(highs - high[None]), axis=0)
        log_total = jnp.log(total)
        lse0 = high[:, 0:1] + log_total[:, 0:1]
        lse1 = high[:, 2:3] + log_total[:, 2:3]
        kl = total[:, 1:2] / total[:, 0:1] - (lse0 - lse1)

        lp0 = l0 - lse0
        diff = lp0 - (l1 - lse1)
        prob = jnp.exp(lp0)
        gbuf[mp, rows_of(0), :] = (
            coef * (adv_col * (prob - onehot) + kl_coef * prob * (diff - kl))).astype(bf16)
        for i in range(TURNS):
            for who in (0, 1):
                begin_if("active", gs_copy, 0, i, who)

    @pl.when(jnp.logical_not(active))
    def _():
        for i in range(TURNS):
            for who in (0, 1):
                gs_copy(0, i, who).wait_recv()

    def gz_copy(o, i, to):
        view = gbuf.at[mp, rows_of(o), glanes(i, core)]
        return rcopy(view, view, "gz", ((o - to) % nz) * TURNS + i, {"tok": lax.rem(tok + 2 * to + nt, nt)})

    def gz_arrival(o, i):
        view = gbuf.at[mp, rows_of(o), glanes(i, core)]
        return rcopy(view, view, "gz", (o % nz) * TURNS + i, {"tok": tok})

    def gx_copy(o, i):
        view = gbuf.at[1, rows_of(o), glanes(i, core)]
        return rcopy(view, view, "gx", (o % nz) * TURNS + i, {"mp": 1 - mp})

    def gxs_copy(o, i, who):
        view = gbuf.at[1, rows_of(o), glanes(i, who)]
        return rcopy(view, view, "gxs", (o % nz) * TURNS + i, {"tok": sib})

    def sides(d, i):
        if d == half:
            return (-1,) if i % 2 == 0 else (1,)
        return (-1, 1)

    def over_x(o, i):
        @pl.when(mp == 1)
        def _():
            begin_if("ref", gx_copy, o, i)

    for d in range(1, min(2, half) + 1):
        for i in range(TURNS):
            for side in sides(d, i):
                begin(gz_copy(0, i, -side * d))
    for i in range(TURNS):
        over_x(0, i)

    def along(d):
        for i in range(TURNS):
            for side in sides(d, i):
                o = side * d
                gz_arrival(o, i).wait_recv()
                if d == 2:
                    for more in range(3, half + 1):
                        if side in sides(more, i):
                            begin(gz_copy(o, i, -side * (more - 2)))
                begin(gs_copy(o, i, core))
                over_x(o, i)

    def across(d):
        @pl.when(mp == 0)
        def _():
            for i in range(TURNS):
                for side in sides(d, i) if d else (1,):
                    gx_copy(side * d, i).wait_recv()
                    begin_if("policy", gxs_copy, side * d, i, core)

    def sib_end(i):
        for o in range(1, nz):
            gs_copy(o, i, 1 - core).wait_recv()

    def feature(window, i):
        @pl.when(mp == 0)
        def _():
            if window == 1:
                for o in range(nz):
                    gxs_copy(o, i, 1 - core).wait_recv()
            a, n = turns[i]
            a, n = 2 * a, 2 * n
            skip = over if window == 1 and i == 0 else 0
            first = window * off
            part = lax.dot_general(
                gbuf[window, :, a + skip:a + n], wbuf[:, first + a + skip:first + a + n],
                (((1,), (1,)), ((), ())), preferred_element_type=f32).reshape(nt, 8, width)
            if window == 0 and i == 0:
                fbuf[...] = part
            else:
                fbuf[...] = fbuf[...] + part

    for d in range(1, half + 1):
        along(d)
        if d >= 2:
            across(d - 2)
    across(half - 1)
    for i in range(TURNS):
        sib_end(i)
        feature(0, i)
        if i == 0:
            across(half)
    for i in range(TURNS):
        feature(1, i)

    def fa_copy(j):
        p = lax.rem(tok + j, nt)
        return rcopy(fbuf.at[p], fabuf.at[tok], "fa", j, {"tok": p})

    def fr_copy(j):
        p = lax.rem(voc + j, nv)
        return rcopy(fabuf.at[pl.ds(p * spv, spv)], frbuf.at[voc], "fr", j, {"vocab": p})

    target = voc // (nv // 2)

    def fb_copy(j):
        p = lax.rem(voc + j, nv)
        return rcopy(fbb.at[voc], fbb.at[voc], "fb", j, {"mp": target, "vocab": p})

    def fm_copy(j, other):
        p = lax.rem(voc + j, nv)
        return rcopy(dots.at[voc], dots.at[voc], "fm", other * nv + j, {"mp": other, "vocab": p})

    def due(j):
        return lax.rem(voc - j + nv, nv) // (nv // 2) == mp

    @pl.when(mp == 0)
    def _():
        @pl.loop(1, nt)
        def _(j):
            fa_copy(j).start()

        fabuf[tok] = fbuf[tok]

    for c in (dw_copy, unit_copy, inv_copy):
        c.wait_recv()
    n_half = vocab_dev // 2
    shift = n_half - off

    def hcopy(k):
        return pltpu.make_async_copy(
            hbuf.at[pl.ds(k * kh, kh), :], head_out.at[0, pl.ds(k * kh, kh), :], hsem.at[k])

    def head_rows(k):
        dw = jnp.where(mp == 0, colb[k].astype(f32), dwb[k].astype(f32)).T.astype(bf16)
        for a, n in hpieces:
            n = min(n, n_half - a)

            @pl.when(mp == 0)
            def _():
                hbuf[k * kh:(k + 1) * kh, a:a + n] = jnp.dot(
                    dw, gbuf[0, :, a:a + n], preferred_element_type=f32).astype(bf16)

            @pl.when(mp == 1)
            def _():
                wide = min(n + LANES, W - a)
                hbuf[k * kh:(k + 1) * kh, a:a + n] = jnp.dot(
                    dw, gbuf[1, :, a:a + wide][:, shift:shift + n], preferred_element_type=f32).astype(bf16)
        hcopy(k).start()

    head_rows(0)

    @pl.when(mp == 0)
    def _():
        @pl.loop(1, nt)
        def _(j):
            fa_copy(j).wait_recv()

        @pl.loop(1, nv)
        def _(j):
            fr_copy(j).start()

        frbuf[voc] = fabuf[pl.ds(voc * spv, spv)]

    head_rows(1)

    @pl.when(mp == 0)
    def _():
        @pl.loop(1, nv)
        def _(j):
            fr_copy(j).wait_recv()

        scaled = jnp.sum(frbuf[...], axis=0) * gainb[pl.ds(voc * spv, spv)]
        mine = ubuf[pl.ds(voc * spv, spv)] * scaled
        dot = jnp.sum(jnp.sum(mine, axis=2, keepdims=True), axis=0)
        fbb[voc] = scaled
        dots[voc] = jnp.broadcast_to(dot, (8, LANES))

        @pl.loop(1, nv)
        def _(j):
            fb_copy(j).start()
            fm_copy(j, 0).start()
            fm_copy(j, 1).start()

        fm_copy(0, 1).start()

        @pl.when(target == 1)
        def _():
            fb_copy(0).start()

        @pl.loop(1, nv)
        def _(j):
            fm_copy(j, 0).wait_recv()

            @pl.when(due(j))
            def _():
                fb_copy(j).wait_recv()

    @pl.when(mp == 1)
    def _():
        @pl.loop(0, nv)
        def _(j):
            fm_copy(j, 1).wait_recv()

            @pl.when(due(j))
            def _():
                fb_copy(j).wait_recv()

    mean = jnp.sum(dots[...], axis=0)[:, 0:1] * (1.0 / (nt * width))
    inv_pol = jnp.where(mp == 0, ibuf[:, 0:1], irecv[:, 0:1])
    for i in range(nt // 2):
        slab = mp * (nt // 2) + i
        unit_pol = jnp.where(mp == 0, ubuf[i], urecv[i])
        hg_out[:, i * width:(i + 1) * width] = inv_pol * (
            fbb[slab // spv, lax.rem(slab, spv)] - unit_pol * mean)

    for k in range(2):
        hcopy(k).wait()
    for c in pending:
        c.wait_send()

    @pl.loop(1, nt)
    def _(j):
        a2a_copy(j).wait_send()
        meta_copy(j).wait_send()

    @pl.when(active)
    def _():
        stat_copy(1, 0).wait_send()

        @pl.loop(1, nv)
        def _(j):
            stat_copy(0, j).wait_send()
            stat_copy(1, j).wait_send()

    for name, cond in (
            ("active", active), ("idle", jnp.logical_not(active)), ("ref", mp == 1), ("policy", mp == 0)):
        @pl.when(cond)
        def _():
            for make, at in held[name]:
                make(*at).wait_send()

    @pl.when(mp == 0)
    def _():
        @pl.loop(1, nt)
        def _(j):
            fa_copy(j).wait_send()

        @pl.loop(1, nv)
        def _(j):
            fr_copy(j).wait_send()
            fb_copy(j).wait_send()
            fm_copy(j, 0).wait_send()
            fm_copy(j, 1).wait_send()

        fm_copy(0, 1).wait_send()

        @pl.when(target == 1)
        def _():
            fb_copy(0).wait_send()


def per_device(nt, nv, hidden, norm_gain, output_head, token_ids, live_mask, advantages):
    nz = nt // 2
    half = nz // 2
    rows, width = output_head.shape[1:]
    kh = width // 2
    blocks = rows // LANES
    W = (blocks + 1) // 2 * LANES
    piece = pieces_of(W // LANES, RING)[0][1]
    T = nt * 8
    spv = nt // nv
    plan, n_sem = sem_plan(nt, nz, nv)
    vmem = pl.BlockSpec(memory_space=pltpu.VMEM)
    smem = pl.BlockSpec(memory_space=pltpu.SMEM)
    hbm = pl.BlockSpec(memory_space=pl.ANY)
    V = pltpu.VMEM
    hg, head_part = pl.pallas_call(
        functools.partial(kernel, nt, nz, nv, plan),
        out_shape=(
            jax.ShapeDtypeStruct((8, nt // 2 * width), f32),
            jax.ShapeDtypeStruct((1, width, rows // 2), bf16),
        ),
        in_specs=[vmem, vmem, hbm, smem, smem, smem],
        out_specs=(vmem, hbm),
        scratch_shapes=[
            V((width, rows), bf16),
            V((RING, T, piece), f32),
            V((RING, T, piece), f32),
            V((RING, T, piece), f32),
            V((2, half, RING, 16, piece), f32),
            V((RING, 16, piece), f32),
            V((2, T, W), bf16),
            V((width, rows // 2), bf16),
            V((nt, 16, kh), bf16),
            V((nt, 16, kh), bf16),
            V((nt, 8, width), f32),
            V((nt // 2, 8, width), f32),
            V((8, LANES), f32),
            V((8, LANES), f32),
            V((nt, 8, width), f32),
            V((nt, 8, LANES), f32),
            V((2, T, kh), bf16),
            V((2, T, kh), bf16),
            V((2 * nv, 2, 16, LANES), f32),
            V((nt, 8, width), f32),
            V((nt, 8, width), f32),
            V((nv, spv, 8, width), f32),
            V((nv, spv, 8, width), f32),
            V((nv, 8, LANES), f32),
            pltpu.SemaphoreType.DMA((2,)),
            pltpu.SemaphoreType.DMA((2,)),
            pltpu.SemaphoreType.DMA((n_sem,)),
            pltpu.SemaphoreType.DMA((n_sem,)),
        ],
        compiler_params=pltpu.CompilerParams(
            collective_id=0, has_side_effects=True, vmem_limit_bytes=56 * 2**20),
        cost_estimate=pl.CostEstimate(
            flops=5 * rows * width * T, bytes_accessed=3 * rows * width, transcendentals=3 * 16 * W),
    )(hidden, norm_gain, jnp.swapaxes(output_head, 1, 2), token_ids, live_mask, advantages)
    return hg, jnp.swapaxes(head_part, 1, 2)


def solution(mesh):
    placed = (
        P("mp", "tok", None),
        P("mp", None),
        P("mp", "vocab", "tok"),
        P("tok"),
        P("tok"),
        P("tok"),
    )
    return jax.shard_map(
        functools.partial(per_device, mesh.shape["tok"], mesh.shape["vocab"]),
        mesh=mesh,
        in_specs=placed,
        out_specs=(P("tok", "mp"), P("mp", "vocab", "tok")),
        check_vma=False,
    )
```
